512 devices in a mesh: head: 4 (over z_lo, core), inner: 8 (over y), outer: 16 (over z_hi, x).
Axes of the slice: x: 4, y: 8, z: 8 (z_hi: 4, z_lo: 2; z = z_hi * 2 + z_lo), core: 2. Of those that a mesh axis runs over, the one named last changes fastest.
Arguments:
- queries: bfloat16 [16384, 6144], P(('outer', 'inner', 'head')), may hold values from -6 to 6
- keys: bfloat16 [16384, 1024], P(('outer', 'inner', 'head')), may hold values from -6 to 6
- values: bfloat16 [16384, 1024], P(('outer', 'inner', 'head')), may hold values from -6 to 6
- grad_out: bfloat16 [16384, 6144], P(('outer', 'inner', 'head')), may hold values from -6 to 6
- positions: int32 [16384], P(('outer', 'inner')), may hold values from 0 to 16383, as said below
Outputs:
- grad_queries: bfloat16 [16384, 6144], P(('outer', 'inner', 'head'))
- grad_keys: bfloat16 [16384, 1024], P(('outer', 'inner', 'head'))
- grad_values: bfloat16 [16384, 1024], P(('outer', 'inner', 'head'))
The draws below stay inside these ranges and needn't reach their ends.
Inputs may be any that keep to these rules, and one draw needn't show every extreme that they name: Rows o * 1024 to (o + 1) * 1024 - 1 hold a permutation of the positions o * 1024 to (o + 1) * 1024 - 1, in aligned runs of 64 rows whose positions are consecutive and increasing.
All inputs are finite; a program needn't handle non-finite values.
Results may differ from the reference program's by a relative error of at most 0.019.
Values may be sent and summed in bfloat16 or wider, within the bound.
A program may use at most 64 MiB of HBM per device.

```python
import jax
import jax.numpy as jnp
from jax import lax

D_HEAD = 128
QH = 48
KVH = 8
TOK_CYCLE = 128
BLOCK_LEN = 1024
TOKENS = 16384


def draw_keys(key, part):
    key = jax.random.fold_in(key, 3)
    result = jnp.clip(jax.random.normal(key, (TOKENS, KVH, D_HEAD), jnp.float32), -6.0, 6.0)
    return result.reshape(TOKENS, KVH * D_HEAD).astype(jnp.bfloat16)


def draw_queries(key, part):
    key = jax.random.fold_in(key, 5)
    per_group = QH // KVH
    result = jnp.clip(jax.random.normal(key, (TOKENS, KVH, per_group, D_HEAD), jnp.float32), -6.0, 6.0)
    return result.reshape(TOKENS, QH * D_HEAD).astype(jnp.bfloat16)


def draw_positions(key, part):
    key = jax.random.fold_in(key, 7)
    outer_count = TOKENS // BLOCK_LEN
    slot_count = 2 * (BLOCK_LEN // TOK_CYCLE)
    half_len = TOK_CYCLE // 2
    orders = jax.vmap(lambda piece: jax.random.permutation(piece, slot_count))(jax.random.split(key, outer_count))
    starts = jnp.arange(outer_count, dtype=jnp.int32)[:, None, None] * BLOCK_LEN
    starts = starts + orders[:, :, None].astype(jnp.int32) * half_len
    starts = starts + jnp.arange(half_len, dtype=jnp.int32)[None, None, :]
    return starts.reshape(TOKENS).astype(jnp.int32)


def shard_levels(stream_key, shape, pieces, least, top_value):
    def one(position, blocks):
        steps = jax.random.uniform(jax.random.fold_in(jax.random.fold_in(stream_key, 6), position), (blocks,), jnp.float32, least / len(pieces), top_value / len(pieces))
        return jnp.repeat(jnp.exp(steps), shape[position] // blocks).reshape((-1,) + (1,) * (len(shape) - position - 1))

    loudness = one(*pieces[0])
    for cut in pieces[1:]:
        loudness = loudness * one(*cut)
    return loudness


def gaussian(own_key, dims, spread, limit, shards=(), kind=jnp.bfloat16):
    values = spread * jax.random.normal(own_key, dims, jnp.float32)
    if shards:
        values = values * shard_levels(own_key, dims, shards, -0.22, 0.18)
    return jnp.clip(values, -limit, limit).astype(kind)


def setup_inputs(seed: int = 0) -> dict:
    seeds = jax.random.split(jax.random.key(seed), 6)
    queries = draw_queries(jax.random.fold_in(seeds[5], 71), 0)
    keys = draw_keys(jax.random.fold_in(seeds[5], 71), 0)
    values = gaussian(seeds[2], (TOKENS, KVH * D_HEAD), 1.0, 6.0, ((0, 512),))
    grad_out = gaussian(seeds[3], (TOKENS, QH * D_HEAD), 1.0, 6.0, ((0, 512),))
    positions = draw_positions(jax.random.fold_in(seeds[5], 71), 0)
    return {"queries": queries, "keys": keys, "values": values, "grad_out": grad_out, "positions": positions}


def reference(queries, keys, values, grad_out, positions):
    softmax_scale = D_HEAD ** -0.5
    per_group = QH // KVH
    block_count = TOKENS // BLOCK_LEN
    highest = lax.Precision.HIGHEST

    def heads_first(tensor):
        shaped = tensor.reshape(block_count, BLOCK_LEN, KVH, per_group, D_HEAD)
        return shaped.transpose(0, 2, 1, 3, 4).reshape(block_count * KVH, BLOCK_LEN, per_group, D_HEAD)

    def paired(tensor):
        shaped = tensor.reshape(block_count, BLOCK_LEN, KVH, D_HEAD)
        both = jnp.concatenate([jnp.roll(shaped, 1, axis=0), shaped], axis=1)
        return both.transpose(0, 2, 1, 3).reshape(block_count * KVH, 2 * BLOCK_LEN, D_HEAD)

    query_all = heads_first(queries)
    upstream_all = heads_first(grad_out)
    key_all = paired(keys)
    value_all = paired(values)
    block_pos = positions.reshape(block_count, BLOCK_LEN)
    query_pos = jnp.repeat(block_pos, KVH, axis=0)
    key_pos = jnp.repeat(jnp.concatenate([jnp.roll(block_pos, 1, axis=0), block_pos], axis=1), KVH, axis=0)

    def one_block(operands):
        query_blk, key_blk, value_blk, upstream_blk, qpos_blk, kpos_blk = operands
        query_f = query_blk.astype(jnp.float32)
        key_f = key_blk.astype(jnp.float32)
        value_f = value_blk.astype(jnp.float32)
        upstream_f = upstream_blk.astype(jnp.float32)
        logits = jnp.einsum("qgd,kd->gqk", query_f, key_f, precision=highest) * softmax_scale
        allowed = (kpos_blk[None, :] <= qpos_blk[:, None]) & (qpos_blk[:, None] // BLOCK_LEN - kpos_blk[None, :] // BLOCK_LEN <= 1)
        masked = jnp.where(allowed[None], logits, -jnp.inf)
        row_max = jnp.max(masked, axis=-1, keepdims=True)
        lse = row_max + jnp.log(jnp.sum(jnp.exp(masked - row_max), axis=-1, keepdims=True))
        probs = jnp.where(allowed[None], jnp.exp(logits - lse), 0.0)
        probs_half = lax.optimization_barrier(probs.astype(jnp.bfloat16)).astype(jnp.float32)
        attended = jnp.einsum("gqk,kd->gqd", probs_half, value_f, precision=highest)
        row_delta = jnp.sum(attended * upstream_f.transpose(1, 0, 2), axis=-1, keepdims=True)
        dprobs = jnp.einsum("qgd,kd->gqk", upstream_f, value_f, precision=highest)
        dscores = probs * (dprobs - row_delta)
        dscores_half = lax.optimization_barrier(dscores.astype(jnp.bfloat16)).astype(jnp.float32)
        grad_q = jnp.einsum("gqk,kd->qgd", dscores_half, key_f, precision=highest) * softmax_scale
        grad_k = jnp.einsum("gqk,qgd->kd", dscores_half, query_f, precision=highest) * softmax_scale
        grad_v = jnp.einsum("gqk,qgd->kd", probs_half, upstream_f, precision=highest)
        return grad_q, grad_k, grad_v

    grad_q, grad_k, grad_v = lax.map(one_block, (query_all, key_all, value_all, upstream_all, query_pos, key_pos))
    grad_q = grad_q.reshape(block_count, KVH, BLOCK_LEN, per_group, D_HEAD).transpose(0, 2, 1, 3, 4)
    grad_q = grad_q.reshape(TOKENS, QH * D_HEAD)

    def folded(terms):
        shaped = terms.reshape(block_count, KVH, 2 * BLOCK_LEN, D_HEAD)
        summed = shaped[:, :, BLOCK_LEN:] + jnp.roll(shaped[:, :, :BLOCK_LEN], -1, axis=0)
        return summed.transpose(0, 2, 1, 3).reshape(TOKENS, KVH * D_HEAD)

    return (grad_q.astype(jnp.bfloat16), folded(grad_k).astype(jnp.bfloat16), folded(grad_v).astype(jnp.bfloat16))
```

```python
import functools

import jax
import jax.numpy as jnp
from jax import lax
from jax.experimental import pallas as pl
from jax.experimental.pallas import tpu as pltpu
from jax.sharding import PartitionSpec as P

D = 128
RUN = 64
NX = 4
KVH = 8
MESH = pl.DeviceIdType.MESH
NEG = -1e30
SCALE = D ** -0.5
EXP_SCALE = SCALE * 1.4426950408889634
F32 = jnp.float32
BF16 = jnp.bfloat16


def dot(a, b):
    return lax.dot_general(a, b, (((1,), (0,)), ((), ())), preferred_element_type=F32)


def sum8(value):
    rows, width = value.shape
    return jnp.sum(value.reshape(rows // 8, 8, width), axis=0)


def kernel(
    ny, nzh, group,
    q_ref, k_ref, v_ref, go_ref, pos_ref,
    gq_ref, gk_ref, gv_ref,
    kv, qbuf, gbuf, poss, qrow, grow, q_t, g_t, pst, dpst, mst, mrun, lrun, drun, dq_t,
    acc, part, rbuf, prior_out, prior_in, kv_out, gq_out,
    fs, fr, ns, nr, ms, mr, ps, pr, hs, hr, rs, rr, bs, br,
):
    half = ny // 2
    width = group * D
    hd, y, o = lax.axis_index("head"), lax.axis_index("inner"), lax.axis_index("outer")
    zl, c = lax.div(hd, 2), lax.rem(hd, 2)
    zh, x = lax.div(o, NX), lax.rem(o, NX)
    xc, s = lax.div(x, 2), lax.rem(x, 2)
    kvh = zl * NX + x
    own = c == xc
    y_right, y_left = lax.rem(y + 1, ny), lax.rem(y + ny - 1, ny)

    forward = []
    for a in range(2):
        for b in range(NX):
            zl2, x2 = lax.rem(zl + a, 2), lax.rem(x + b, NX)
            forward.append(((zl2 * 2 + xc, y, zh * NX + x2), zl2 * NX + x2, own if a + b == 0 else None))
    back = []
    for i in range(4):
        for s2 in range(2):
            hd2 = lax.rem(hd + i, 4)
            me = (2 * c + s2 == x) if i == 0 else None
            back.append(((hd2, y, zh * NX + 2 * c + s2), hd2, s2, me))
    sibling = hd + 1 - 2 * c
    after = (sibling, y, lax.rem(zh + c, nzh) * NX + x)
    before = (sibling, y, lax.rem(zh + nzh - 1 + c, nzh) * NX + x)
    right, left = (hd, y_right, o), (hd, y_left, o)

    def remote(src, dst, send, recv, device):
        return pltpu.make_async_remote_copy(
            src_ref=src, dst_ref=dst, send_sem=send, recv_sem=recv, device_id=device, device_id_type=MESH
        )

    def start(src, dst, send, recv, device, me):
        if me is None:
            remote(src, dst, send, recv, device).start()
        else:
            @pl.when(me)
            def _():
                pltpu.make_async_copy(src, dst, recv).start()

            @pl.when(jnp.logical_not(me))
            def _():
                remote(src, dst, send, recv, device).start()

    def wait_send(src, dst, send, recv, device, me):
        if me is None:
            remote(src, dst, send, recv, device).wait_send()
        else:
            @pl.when(jnp.logical_not(me))
            def _():
                remote(src, dst, send, recv, device).wait_send()

    def wait_recv(dst, recv):
        remote(dst, dst, recv, recv, right).wait_recv()

    barrier = pltpu.get_barrier_semaphore()

    def greet(device):
        pl.semaphore_signal(barrier, inc=1, device_id=device, device_id_type=MESH)

    for device, me in [(f[0], f[2]) for f in forward] + [(b[0], b[3]) for b in back]:
        if me is None:
            greet(device)
        else:
            @pl.when(jnp.logical_not(me))
            def _(device=device):
                greet(device)
    for device in (right, left, after, before):
        greet(device)

    run_id = lax.rem(lax.div(pos_ref[...], RUN), 2 * ny).astype(F32)
    poss[...] = jnp.broadcast_to(run_id, poss.shape).astype(BF16)
    pl.semaphore_wait(barrier, 20 - 2 * own.astype(jnp.int32))

    slot = s * 4 + hd
    token_rows = pl.ds(pl.multiple_of(hd * 32, 32), 32)
    kv_rows = pl.ds(pl.multiple_of(128 + s * 128 + hd * 32, 32), 32)

    def pieces(n, kvh2):
        kv_cols = pl.ds(pl.multiple_of(kvh2 * D, D), D)
        q_cols = pl.ds(pl.multiple_of(kvh2 * width, D), width)
        return (
            (k_ref.at[:, kv_cols], kv.at[y, 0, kv_rows, :], fs.at[0, n], fr.at[0, slot]),
            (v_ref.at[:, kv_cols], kv.at[y, 1, kv_rows, :], fs.at[1, n], fr.at[1, slot]),
            (q_ref.at[:, q_cols], qbuf.at[s, token_rows, :], fs.at[2, n], fr.at[2, slot]),
            (go_ref.at[:, q_cols], gbuf.at[s, token_rows, :], fs.at[3, n], fr.at[3, slot]),
            (poss, kv.at[y, s, pl.ds(384, 16), :], fs.at[4, n], fr.at[4, s]),
        )

    for arrays in ((0, 1), (2, 3)):
        for n, (device, kvh2, me) in enumerate(forward):
            for array in arrays:
                start(*pieces(n, kvh2)[array], device, me)
        if arrays[0] == 0:
            @pl.when(hd == 0)
            def _():
                for n, (device, kvh2, me) in enumerate(forward):
                    start(*pieces(n, kvh2)[4], device, me)

    def wait_kv(s2):
        for hd2 in range(4):
            rows = pl.ds(128 + s2 * 128 + hd2 * 32, 32)
            for which in range(2):
                wait_recv(kv.at[y, which, rows, :], fr.at[which, s2 * 4 + hd2])
        wait_recv(kv.at[y, s2, pl.ds(384, 16), :], fr.at[4, s2])

    wait_kv(1)
    onward = (kv.at[y, :, pl.ds(256, 128), :], kv.at[y, :, pl.ds(0, 128), :], ns.at[0], nr.at[0], after)
    remote(*onward).start()
    wait_kv(0)

    def ring_copy(way, d, part_id):
        origin = lax.rem(y + ny + (1 - d if way == 0 else d - 1), ny)
        device = right if way == 0 else left
        if d == half:
            view = kv.at[origin, way]
            return remote(view, view, hs.at[way], hr.at[way], device)
        view = kv.at[origin, :, pl.ds(128, 272), :] if part_id == 0 else kv.at[origin, :, pl.ds(0, 128), :]
        send, recv = (ms, mr) if part_id == 0 else (ps, pr)
        return remote(view, view, send.at[way, d - 1], recv.at[way, d - 1], device)

    def ring_wait(way, d, part_id):
        origin = lax.rem(y + ny + (-d if way == 0 else d), ny)
        if d == half:
            wait_recv(kv.at[origin, way], hr.at[way])
            return
        view = kv.at[origin, :, pl.ds(128, 272), :] if part_id == 0 else kv.at[origin, :, pl.ds(0, 128), :]
        wait_recv(view, (mr if part_id == 0 else pr).at[way, d - 1])

    def ring_step(d):
        if d == half:
            ring_wait(0, d, 0)
            ring_wait(1, d, 0)
            return
        for part_id in range(2):
            for way in range(2):
                ring_wait(way, d, part_id)
                if d + 1 < half:
                    ring_copy(way, d + 1, part_id).start()
                elif part_id == 1:
                    ring_copy(way, d + 1, 0).start()

    ring_copy(0, 1, 0).start()
    ring_copy(1, 1, 0).start()
    wait_recv(kv.at[y, :, pl.ds(0, 128), :], nr.at[0])
    ring_copy(0, 1, 1).start()
    ring_copy(1, 1, 1).start()
    ring_step(1)

    for s2 in range(2):
        for hd2 in range(4):
            wait_recv(qbuf.at[s2, pl.ds(hd2 * 32, 32), :], fr.at[2, s2 * 4 + hd2])
            wait_recv(gbuf.at[s2, pl.ds(hd2 * 32, 32), :], fr.at[3, s2 * 4 + hd2])
        for g in range(group):
            cols = slice(g * D, (g + 1) * D)
            for src, rows_ref, t_ref in ((qbuf, qrow, q_t), (gbuf, grow, g_t)):
                piece = src[s2, :, cols]
                rows_ref[s2, cols, :] = piece
                t_ref[s2, :, cols] = piece.T

    mrun[...] = jnp.full(mrun.shape, NEG, F32)
    lrun[...] = jnp.zeros(lrun.shape, F32)
    drun[...] = jnp.zeros(drun.shape, F32)
    dq_t[...] = jnp.zeros(dq_t.shape, F32)

    first = jnp.logical_and(c == 0, zh == 0)
    penalties = (jnp.where(first, -NEG, 0.0), None)
    key_off = lax.rem(lax.broadcasted_iota(jnp.int32, (128, 128), 0), RUN).astype(F32)
    row_off = lax.rem(lax.broadcasted_iota(jnp.int32, (8, 128), 1), RUN).astype(F32)

    def forward_chunk(origin):
        for qb in range(2):
            keys = kv[origin, 0, pl.ds(qb * 128, 256), :]
            vals = kv[origin, 1, pl.ds(qb * 128, 256), :]
            scores = dot(keys, q_t[qb])
            dprobs = dot(vals, g_t[qb])
            dpst[origin, qb] = dprobs
            runs = kv[origin, qb, pl.ds(384, 16), :].astype(F32)[:1, :]
            key_pos = jnp.broadcast_to(runs, (128, 128)).T * RUN + key_off
            row_runs = kv[y, qb, pl.ds(384, 16), :].astype(F32)[:1, :]
            allowed = key_pos <= row_runs * RUN + row_off[:1, :]
            prior = scores[:128]
            near = jnp.concatenate(
                [jnp.where(allowed, scores[128:, g * D:(g + 1) * D], NEG) for g in range(group)], axis=1
            )
            prior_top = jnp.max(prior, axis=0, keepdims=True)
            if penalties[qb] is not None:
                prior_top = prior_top - penalties[qb]
            old = mrun[qb]
            top = jnp.maximum(old, jnp.maximum(prior_top, jnp.max(near, axis=0, keepdims=True)))
            mrun[qb] = top
            mst[origin, qb] = top
            shift = top * EXP_SCALE
            prior_shift = shift if penalties[qb] is None else shift + penalties[qb]
            probs = jnp.concatenate(
                [jnp.exp2(prior * EXP_SCALE - prior_shift), jnp.exp2(near * EXP_SCALE - shift)], axis=0
            )
            faded = jnp.exp2((old - top) * EXP_SCALE)
            lrun[qb] = lrun[qb] * faded + sum8(probs)
            drun[qb] = drun[qb] * faded + sum8(probs * dprobs)
            pst[origin, qb] = probs.astype(BF16)

    def chunk_at(d, j):
        return lax.rem(y + ny + (1 - 2 * j) * d, ny)

    def pair(d, work):
        lax.fori_loop(0, 2, lambda j, _: (work(j, chunk_at(d, j)), 0)[1], 0)

    forward_chunk(y)
    pair(1, lambda j, origin: forward_chunk(origin))
    for d in range(2, half):
        ring_step(d)
        pair(d, lambda j, origin: forward_chunk(origin))
    ring_step(half)
    forward_chunk(chunk_at(half, 0))

    for qb in range(2):
        inverse = 1.0 / jnp.sum(lrun[qb], axis=0, keepdims=True)
        delta = jnp.sum(drun[qb], axis=0, keepdims=True) * inverse
        lrun[qb] = jnp.broadcast_to(inverse, lrun.shape[1:])
        drun[qb] = jnp.broadcast_to(delta, drun.shape[1:])

    def backward_chunk(j, origin):
        terms = []
        for qb in range(2):
            weight = jnp.exp2((mst[origin, qb] - mrun[qb]) * EXP_SCALE) * lrun[qb, :1, :]
            probs = pst[origin, qb].astype(F32) * weight
            dscores = (probs * (dpst[origin, qb] - drun[qb, :1, :])).astype(BF16)
            value_term = dot(probs.astype(BF16), grow[qb])
            key_term = dot(dscores, qrow[qb]) * SCALE
            keys = kv[origin, 0, pl.ds(qb * 128, 256), :]
            dq_t[qb] += dot(keys.T, dscores)
            terms.append((key_term, value_term))
        for which in range(2):
            one, two = terms[0][which], terms[1][which]
            acc[j, which, :128, :] = one[:128]
            acc[j, which, 128:256, :] = one[128:] + two[:128]
            acc[j, which, 256:, :] = two[128:]

    backward_chunk(0, chunk_at(half, 0))
    part[0, 0] = acc[0].astype(BF16)
    opposite = [
        remote(part.at[0, 0, way], rbuf.at[way, 0, way], rs.at[way, 0], rr.at[way, 0], right if way == 0 else left)
        for way in range(2)
    ]
    for copy in opposite:
        copy.start()
    steps = []
    for n in range(1, half):
        pair(half - n, backward_chunk)
        for way in range(2):
            if n == 1:
                wait_recv(rbuf.at[way, 0, way], rr.at[way, 0])
                part[way, n, way] = (acc[way, way] + rbuf[way, 0, way].astype(F32)).astype(BF16)
                part[way, n, 1 - way] = acc[way, 1 - way].astype(BF16)
            else:
                wait_recv(rbuf.at[way, n - 1], rr.at[way, n - 1])
                part[way, n] = (acc[way] + rbuf[way, n - 1].astype(F32)).astype(BF16)
            copy = remote(
                part.at[way, n], rbuf.at[way, n], rs.at[way, n], rr.at[way, n], right if way == 0 else left
            )
            copy.start()
            steps.append(copy)
    backward_chunk(0, y)

    for s2 in range(2):
        for g in range(group):
            cols = slice(g * D, (g + 1) * D)
            gq_out[s2, :, cols] = (dq_t[s2, :, cols].T * SCALE).astype(BF16)
    q_cols = pl.ds(pl.multiple_of(kvh * width, D), width)
    kv_cols = pl.ds(pl.multiple_of(kvh * D, D), D)

    def back_pieces(n, hd2, s2):
        rows = pl.ds(pl.multiple_of(hd2 * 32, 32), 32)
        return (
            (kv_out.at[0, s2, rows, :], gk_ref.at[:, kv_cols], bs.at[0, n], br.at[0, kvh]),
            (kv_out.at[1, s2, rows, :], gv_ref.at[:, kv_cols], bs.at[1, n], br.at[1, kvh]),
            (gq_out.at[s2, rows, :], gq_ref.at[:, q_cols], bs.at[2, n], br.at[2, kvh]),
        )

    for n, (device, hd2, s2, me) in enumerate(back):
        start(*back_pieces(n, hd2, s2)[2], device, me)

    for way in range(2):
        wait_recv(rbuf.at[way, half - 1], rr.at[way, half - 1])
    total = acc[0] + rbuf[0, half - 1].astype(F32) + rbuf[1, half - 1].astype(F32)
    prior_out[...] = total[:, :128].astype(BF16)
    prior_copy = remote(prior_out, prior_in, ns.at[1], nr.at[1], before)
    prior_copy.start()
    kv_out[:, 0] = total[:, 128:256].astype(BF16)
    acc[0, :, 256:, :] = total[:, 256:]
    for slot2 in range(2):
        if slot2 == 1:
            prior_copy.wait_recv()
            kv_out[:, 1] = (acc[0, :, 256:, :] + prior_in[...].astype(F32)).astype(BF16)
        for n, (device, hd2, s2, me) in enumerate(back):
            if s2 == slot2:
                for array in range(2):
                    start(*back_pieces(n, hd2, s2)[array], device, me)

    for n, (device, kvh2, me) in enumerate(forward):
        for array in range(4):
            wait_send(*pieces(n, kvh2)[array], device, me)

    @pl.when(hd == 0)
    def _():
        for n, (device, kvh2, me) in enumerate(forward):
            wait_send(*pieces(n, kvh2)[4], device, me)

    for d in range(1, half):
        for way in range(2):
            for part_id in range(2):
                ring_copy(way, d, part_id).wait_send()
    for way in range(2):
        ring_copy(way, half, 0).wait_send()
    for copy in opposite + steps + [remote(*onward), prior_copy]:
        copy.wait_send()
    for n, (device, hd2, s2, me) in enumerate(back):
        for array in range(3):
            wait_send(*back_pieces(n, hd2, s2)[array], device, me)
    for kvh2 in range(KVH):
        wait_recv(gk_ref.at[:, pl.ds(kvh2 * D, D)], br.at[0, kvh2])
        wait_recv(gv_ref.at[:, pl.ds(kvh2 * D, D)], br.at[1, kvh2])
        wait_recv(gq_ref.at[:, pl.ds(kvh2 * width, width)], br.at[2, kvh2])


def on_device(queries, keys, values, grad_out, positions):
    ny, nzh = lax.axis_size("inner"), lax.axis_size("outer") // NX
    rows, width = queries.shape
    group = width // (KVH * D)
    half = ny // 2
    lanes = group * D
    anywhere = pl.BlockSpec(memory_space=pl.ANY)
    vmem = pl.BlockSpec(memory_space=pltpu.VMEM)
    dma = pltpu.SemaphoreType.DMA
    return pl.pallas_call(
        functools.partial(kernel, ny, nzh, group),
        out_shape=tuple(jax.ShapeDtypeStruct(a.shape, BF16) for a in (queries, keys, values)),
        in_specs=[anywhere] * 4 + [vmem],
        out_specs=(anywhere,) * 3,
        scratch_shapes=[
            pltpu.VMEM((ny, 2, 400, D), BF16),
            pltpu.VMEM((2, 128, lanes), BF16),
            pltpu.VMEM((2, 128, lanes), BF16),
            pltpu.VMEM((16, 128), BF16),
            pltpu.VMEM((2, lanes, D), BF16),
            pltpu.VMEM((2, lanes, D), BF16),
            pltpu.VMEM((2, D, lanes), BF16),
            pltpu.VMEM((2, D, lanes), BF16),
            pltpu.VMEM((ny, 2, 256, lanes), BF16),
            pltpu.VMEM((ny, 2, 256, lanes), F32),
            pltpu.VMEM((ny, 2, 1, lanes), F32),
            pltpu.VMEM((2, 1, lanes), F32),
            pltpu.VMEM((2, 8, lanes), F32),
            pltpu.VMEM((2, 8, lanes), F32),
            pltpu.VMEM((2, D, lanes), F32),
            pltpu.VMEM((2, 2, 384, D), F32),
            pltpu.VMEM((2, half, 2, 384, D), BF16),
            pltpu.VMEM((2, half, 2, 384, D), BF16),
            pltpu.VMEM((2, 128, D), BF16),
            pltpu.VMEM((2, 128, D), BF16),
            pltpu.VMEM((2, 2, 128, D), BF16),
            pltpu.VMEM((2, 128, lanes), BF16),
            dma((5, 8)), dma((5, 8)),
            dma((2,)), dma((2,)),
            dma((2, half)), dma((2, half)),
            dma((2, half)), dma((2, half)),
            dma((2,)), dma((2,)),
            dma((2, half)), dma((2, half)),
            dma((3, 8)), dma((3, 8)),
        ],
        compiler_params=pltpu.CompilerParams(
            collective_id=0, has_side_effects=True, vmem_limit_bytes=56 * 1024 * 1024
        ),
        name="banded_backward",
    )(queries, keys, values, grad_out, positions.reshape(1, -1))


def solution(mesh):
    tokens = P(("outer", "inner", "head"), None)
    return jax.shard_map(
        on_device,
        mesh=mesh,
        in_specs=(tokens, tokens, tokens, tokens, P(("outer", "inner"))),
        out_specs=(tokens, tokens, tokens),
        check_vma=False,
    )
```

```python
import functools

import jax
import jax.numpy as jnp
from jax import lax
from jax.experimental import pallas as pl
from jax.experimental.pallas import tpu as pltpu
from jax.sharding import PartitionSpec as P

D = 128
RUN = 64
NX = 4
KVH = 8
MESH = pl.DeviceIdType.MESH
NEG = -1e30
SCALE = D ** -0.5
EXP_SCALE = SCALE * 1.4426950408889634
F32 = jnp.float32
BF16 = jnp.bfloat16


def dot(a, b):
    return lax.dot_general(a, b, (((1,), (0,)), ((), ())), preferred_element_type=F32)


def sum8(value):
    rows, width = value.shape
    return jnp.sum(value.reshape(rows // 8, 8, width), axis=0)


def kernel(
    ny, nzh, group,
    q_ref, k_ref, v_ref, go_ref, pos_ref,
    gq_ref, gk_ref, gv_ref,
    kst, vst, staged, poss, kv, qbuf, gbuf, qrow, grow, q_t, g_t, pst, dpst, mst, mrun, lrun, drun, dq_t,
    acc, part, rbuf, sib_out, sib_in, kv_out, kv_in, prior_in, gq_out,
    ls, fs, fr, os, orr, ks, hs, hr, rs, rr, ss, sr, bs, br, ps, pr,
):
    half = ny // 2
    width = group * D
    hd, y, o = lax.axis_index("head"), lax.axis_index("inner"), lax.axis_index("outer")
    zl, c = lax.div(hd, 2), lax.rem(hd, 2)
    zh, x = lax.div(o, NX), lax.rem(o, NX)
    xc, s = lax.div(x, 2), lax.rem(x, 2)
    kvh = zl * NX + x
    own = c == xc
    core0, core1, last_x = c == 0, c == 1, x == NX - 1

    forward = []
    for a in range(2):
        for b in range(NX):
            zl2, x2 = lax.rem(zl + a, 2), lax.rem(x + b, NX)
            forward.append(((zl2 * 2 + xc, y, zh * NX + x2), zl2 * NX + x2, x2, own if a + b == 0 else None))
    back = []
    for i in range(4):
        for s2 in range(2):
            hd2 = lax.rem(hd + i, 4)
            me = (2 * c + s2 == x) if i == 0 else None
            back.append(((hd2, y, zh * NX + 2 * c + s2), hd2, s2, me))
    zh_after, zh_before = lax.rem(zh + 1, nzh), lax.rem(zh + nzh - 1, nzh)
    heirs = [((2 * zl2, y, zh_after * NX + x2), zl2 * NX + x2) for zl2 in range(2) for x2 in range(NX)]
    donors = [((hd2, y, zh_before * NX + NX - 1), hd2) for hd2 in range(4)]
    sibling = (hd + 1 - 2 * c, y, o)
    ring = ((hd, lax.rem(y + 1, ny), o), (hd, lax.rem(y + ny - 1, ny), o))

    def remote(src, dst, send, recv, device):
        return pltpu.make_async_remote_copy(
            src_ref=src, dst_ref=dst, send_sem=send, recv_sem=recv, device_id=device, device_id_type=MESH
        )

    def wait_recv(dst, recv):
        remote(dst, dst, recv, recv, ring[0]).wait_recv()

    sent = []

    def send(src, dst, send_sem, recv_sem, device, me=None):
        copy = remote(src, dst, send_sem, recv_sem, device)
        if me is None:
            copy.start()
            sent.append((copy, None))
        else:
            @pl.when(me)
            def _():
                pltpu.make_async_copy(src, dst, recv_sem).start()

            away = jnp.logical_not(me)

            @pl.when(away)
            def _():
                copy.start()

            sent.append((copy, away))

    def send_if(condition, *copies):
        copies = [remote(*copy) for copy in copies]

        @pl.when(condition)
        def _():
            for copy in copies:
                copy.start()

        sent.extend((copy, condition) for copy in copies)

    barrier = pltpu.get_barrier_semaphore()

    def greet(device):
        pl.semaphore_signal(barrier, inc=1, device_id=device, device_id_type=MESH)

    @pl.when(last_x)
    def _():
        for device, _ in heirs:
            greet(device)

    @pl.when(core0)
    def _():
        for device, _ in donors:
            greet(device)

    for device, me in [(f[0], f[3]) for f in forward] + [(b[0], b[3]) for b in back]:
        if me is None:
            greet(device)
        else:
            @pl.when(jnp.logical_not(me))
            def _(device=device):
                greet(device)
    for device in ring:
        greet(device)

    loads = [pltpu.make_async_copy(src, dst, ls.at[i]) for i, (src, dst) in enumerate(((k_ref, kst), (v_ref, vst)))]
    for load in loads:
        load.start()
    run_id = lax.rem(lax.div(pos_ref[...], RUN), 2 * ny).astype(F32)
    poss[...] = jnp.broadcast_to(run_id, poss.shape).astype(BF16)
    for load in loads:
        load.wait()
    for h in range(KVH):
        staged[h, :32, :] = kst[:, h * D:(h + 1) * D]
        staged[h, 32:, :] = vst[:, h * D:(h + 1) * D]
    mrun[...] = jnp.full(mrun.shape, NEG, F32)
    lrun[...] = jnp.zeros(lrun.shape, F32)
    drun[...] = jnp.zeros(drun.shape, F32)
    dq_t[...] = jnp.zeros(dq_t.shape, F32)
    pl.semaphore_wait(
        barrier,
        18 - 2 * own.astype(jnp.int32) + 8 * last_x.astype(jnp.int32) + 4 * core0.astype(jnp.int32),
    )

    kv_rows = pl.ds(pl.multiple_of(hd * 64, 64), 64)
    for n, (device, kvh2, x2, me) in enumerate(forward):
        send(staged.at[kvh2], kv.at[y, 1 + s, kv_rows, :], fs.at[0, n], fr.at[0, s * 4 + hd], device, me)
    send_if(last_x, *(
        (staged.at[kvh2], kv.at[y, 0, kv_rows, :], os.at[n], orr.at[hd], device)
        for n, (device, kvh2) in enumerate(heirs)
    ))
    for n, (device, kvh2, x2, me) in enumerate(forward):
        runs = (poss, kv.at[y, 1 + s, pl.ds(256, 16), :], fs.at[3, n], fr.at[3, s], device)
        mine = x2 == hd
        if me is None:
            send_if(mine, runs)
        else:
            @pl.when(jnp.logical_and(mine, me))
            def _(runs=runs):
                pltpu.make_async_copy(runs[0], runs[1], runs[3]).start()

            send_if(jnp.logical_and(mine, jnp.logical_not(me)), runs)

    def view(origin, p, d, way):
        rows = pl.ds(0, 272 if p else 256)
        if d == half:
            rows = pl.ds(0, 128) if way == 0 else pl.ds(128, 144 if p else 128)
        return kv.at[origin, p, rows, :]

    def origin_at(way, d):
        return lax.rem(y + ny + (-d if way == 0 else d), ny)

    def gather_send(way, d, p):
        piece = view(origin_at(way, d - 1), p, d, way)
        copy = (piece, piece, hs.at[way, d - 1, p], hr.at[way, d - 1, p], ring[way])
        if p == 0:
            send_if(core0, copy)
        else:
            send(*copy)

    def hand_over(way, d):
        origin = origin_at(way, d)
        rows = pl.ds(0, 256) if d < half else pl.ds(128 * way, 128)
        send_if(core0, (
            kv.at[origin, 2, rows, :], kv.at[origin, 0, rows, :], ks.at[way, d], hr.at[way, d - 1, 0] if d else orr.at[0],
            sibling,
        ))

    def gather_events(d):
        def event(way, p):
            wait_recv(view(origin_at(way, d), p, d, way), hr.at[way, d - 1, p])
            if d < half:
                gather_send(way, d + 1, p)
            if p == 2:
                hand_over(way, d)

        return [functools.partial(event, way, p) for p in (2, 1, 0) for way in range(2)]

    for p in (2, 1):
        for hd2 in range(4):
            wait_recv(kv.at[y, p, pl.ds(hd2 * 64, 64), :], fr.at[0, (p - 1) * 4 + hd2])
        wait_recv(kv.at[y, p, pl.ds(256, 16), :], fr.at[3, p - 1])
        for way in range(2):
            gather_send(way, 1, p)
        if p == 2:
            hand_over(0, 0)

    @pl.when(core0)
    def _():
        for hd2 in range(4):
            wait_recv(kv.at[y, 0, pl.ds(hd2 * 64, 64), :], orr.at[hd2])

    for way in range(2):
        gather_send(way, 1, 0)

    token_rows = pl.ds(pl.multiple_of(hd * 32, 32), 32)
    for n, (device, kvh2, x2, me) in enumerate(forward):
        q_cols = pl.ds(pl.multiple_of(kvh2 * width, D), width)
        send(q_ref.at[:, q_cols], qbuf.at[s, token_rows, :], fs.at[1, n], fr.at[1, s * 4 + hd], device, me)
        send(go_ref.at[:, q_cols], gbuf.at[s, token_rows, :], fs.at[2, n], fr.at[2, s * 4 + hd], device, me)

    for d in range(1, half - 1):
        for event in gather_events(d):
            event()

    @pl.when(core1)
    def _():
        wait_recv(kv.at[y, 0, pl.ds(0, 256), :], orr.at[0])

    for s2 in range(2):
        for hd2 in range(4):
            wait_recv(qbuf.at[s2, pl.ds(hd2 * 32, 32), :], fr.at[1, s2 * 4 + hd2])
            wait_recv(gbuf.at[s2, pl.ds(hd2 * 32, 32), :], fr.at[2, s2 * 4 + hd2])
        for g in range(group):
            cols = slice(g * D, (g + 1) * D)
            for src, rows_ref, t_ref in ((qbuf, qrow, q_t), (gbuf, grow, g_t)):
                piece = src[s2, :, cols]
                rows_ref[s2, cols, :] = piece
                t_ref[s2, :, cols] = piece.T

    first = jnp.logical_and(core0, zh == 0)
    key_off = lax.rem(lax.broadcasted_iota(jnp.int32, (128, 128), 0), RUN).astype(F32)
    row_off = lax.rem(lax.broadcasted_iota(jnp.int32, (8, 128), 1), RUN).astype(F32)

    def rows_of(origin, qb, which):
        at = [pl.ds(hd2 * 64 + which * 32, 32) for hd2 in range(4)]
        return jnp.concatenate([kv[origin, qb + p, rows, :] for p in range(2) for rows in at], axis=0)

    def forward_chunk(origin):
        def block(qb, _):
            scores = dot(rows_of(origin, qb, 0), q_t[qb])
            dprobs = dot(rows_of(origin, qb, 1), g_t[qb])
            dpst[origin, qb] = dprobs
            runs = kv[origin, qb + 1, pl.ds(256, 16), :].astype(F32)[:1, :]
            key_pos = jnp.broadcast_to(runs, (128, 128)).T * RUN + key_off
            row_runs = kv[y, qb + 1, pl.ds(256, 16), :].astype(F32)[:1, :]
            allowed = key_pos <= row_runs * RUN + row_off[:1, :]
            penalty = jnp.where(jnp.logical_and(first, qb == 0), -NEG, 0.0)
            prior = scores[:128]
            near = jnp.concatenate(
                [jnp.where(allowed, scores[128:, g * D:(g + 1) * D], NEG) for g in range(group)], axis=1
            )
            prior_top = jnp.max(prior, axis=0, keepdims=True) - penalty
            old = mrun[qb]
            top = jnp.maximum(old, jnp.maximum(prior_top, jnp.max(near, axis=0, keepdims=True)))
            mrun[qb] = top
            mst[origin, qb] = top
            shift = top * EXP_SCALE
            probs = jnp.concatenate(
                [jnp.exp2(prior * EXP_SCALE - (shift + penalty)), jnp.exp2(near * EXP_SCALE - shift)], axis=0
            )
            faded = jnp.exp2((old - top) * EXP_SCALE)
            lrun[qb] = lrun[qb] * faded + sum8(probs)
            drun[qb] = drun[qb] * faded + sum8(probs * dprobs)
            pst[origin, qb] = probs.astype(BF16)
            return 0

        lax.fori_loop(0, 2, block, 0)

    def chunk_at(d, j):
        return lax.rem(y + ny + (1 - 2 * j) * d, ny)

    chunks = [(0, 0)] + [(d, j) for d in range(1, half - 1) for j in range(2)]
    events = gather_events(half - 1)
    for i, event in enumerate(events):
        event()
        for d, j in chunks[i * len(chunks) // len(events):(i + 1) * len(chunks) // len(events)]:
            forward_chunk(chunk_at(d, j))
    for j in range(2):
        forward_chunk(chunk_at(half - 1, j))
    for event in gather_events(half):
        event()
    forward_chunk(chunk_at(half, 0))

    for qb in range(2):
        inverse = 1.0 / jnp.sum(lrun[qb], axis=0, keepdims=True)
        delta = jnp.sum(drun[qb], axis=0, keepdims=True) * inverse
        lrun[qb] = jnp.broadcast_to(inverse, lrun.shape[1:])
        drun[qb] = jnp.broadcast_to(delta, drun.shape[1:])

    def backward_chunk(d, j):
        origin = chunk_at(d, j)

        def block(qb, _):
            weight = jnp.exp2((mst[origin, qb] - mrun[qb]) * EXP_SCALE) * lrun[qb, :1, :]
            probs = pst[origin, qb].astype(F32) * weight
            dscores = (probs * (dpst[origin, qb] - drun[qb, :1, :])).astype(BF16)
            acc[origin, qb, 0] = dot(dscores, qrow[qb]) * SCALE
            acc[origin, qb, 1] = dot(probs.astype(BF16), grow[qb])
            dq_t[qb] += dot(rows_of(origin, qb, 0).T, dscores)
            return 0

        lax.fori_loop(0, 2, block, 0)

        @pl.when(core1)
        def _():
            sib_out[origin] = acc[origin, 0, :, :128, :].astype(BF16)

        send_if(core1, (sib_out.at[origin], sib_in.at[origin], ss.at[d, j], sr.at[d, j], sibling))

    def term(d, j, p, which):
        origin = chunk_at(d, j)
        if p == 0:
            return acc[origin, 0, which, :128, :]
        if p == 1:
            return acc[origin, 0, which, 128:, :] + acc[origin, 1, which, :128, :]
        mine = acc[origin, 1, which, 128:, :]
        return mine + jnp.where(core0, sib_in[origin, which].astype(F32), 0.0)

    def from_sibling(d, j):
        @pl.when(core0)
        def _():
            wait_recv(sib_in.at[chunk_at(d, j)], sr.at[d, j])

    def scatter(n, way, p):
        d = half - n
        if n == 1:
            wait_recv(rbuf.at[way, 0, p, way], rr.at[way, 0, p])
        elif n > 1:
            wait_recv(rbuf.at[way, n - 1, p], rr.at[way, n - 1, p])
        for which in range(2):
            if n == 0 and which != way:
                continue
            total = term(d, way if n else 0, p, which)
            if n > 1 or n == 1 and which == way:
                total = total + rbuf[way, n - 1, p, which].astype(F32)
            part[way, n, p, which] = total.astype(BF16)

    def scatter_events(n):
        def event(way, p):
            if p == 2 and (n or not way):
                from_sibling(half - n, way)
            at = (way, n, p) if n else (way, n, p, way)
            copy = (part.at[at], rbuf.at[at], rs.at[way, n, p], rr.at[way, n, p], ring[way])
            if p == 0:
                @pl.when(core0)
                def _():
                    scatter(n, way, p)

                send_if(core0, copy)
            else:
                scatter(n, way, p)
                send(*copy)

        return [functools.partial(event, way, p) for p in range(3) for way in range(2)]

    backward_chunk(half, 0)
    for event in scatter_events(0):
        event()
    for n in range(1, half):
        for d in (half - 1, half - 2) if n == 1 else (half - n - 1,):
            for j in range(2 if d else 1):
                backward_chunk(d, j)
        if n == half - 1:
            for s2 in range(2):
                for g in range(group):
                    cols = slice(g * D, (g + 1) * D)
                    gq_out[s2, :, cols] = (dq_t[s2, :, cols].T * SCALE).astype(BF16)
            q_cols = pl.ds(pl.multiple_of(kvh * width, D), width)
            for m, (device, hd2, s2, me) in enumerate(back):
                rows = pl.ds(pl.multiple_of(hd2 * 32, 32), 32)
                send(gq_out.at[s2, rows, :], gq_ref.at[:, q_cols], bs.at[1, m], br.at[1, kvh], device, me)
        for event in scatter_events(n):
            event()

    def finish(p):
        for way in range(2):
            wait_recv(rbuf.at[way, half - 1, p], rr.at[way, half - 1, p])
        for which in range(2):
            total = term(0, 0, p, which)
            total = total + rbuf[0, half - 1, p, which].astype(F32) + rbuf[1, half - 1, p, which].astype(F32)
            for hd2 in range(4):
                kv_out[p, hd2, pl.ds(which * 32, 32), :] = total[hd2 * 32:(hd2 + 1) * 32].astype(BF16)

    @pl.when(core0)
    def _():
        finish(0)

    send_if(core0, *(
        (kv_out.at[0, hd2], prior_in.at[kvh], ps.at[hd2], pr.at[kvh], device) for device, hd2 in donors
    ))
    for p in (1, 2):
        if p == 2:
            from_sibling(0, 0)
        finish(p)
        for m, (device, hd2, s2, me) in enumerate(back):
            if s2 == p - 1:
                send(kv_out.at[p, hd2], kv_in.at[kvh], bs.at[0, m], br.at[0, kvh], device, me)

    def results(with_prior):
        for h in range(KVH):
            both = kv_in[h]
            if with_prior:
                both = (both.astype(F32) + prior_in[h].astype(F32)).astype(BF16)
            cols = slice(h * D, (h + 1) * D)
            gk_ref[:, cols] = both[:32]
            gv_ref[:, cols] = both[32:]

    for h in range(KVH):
        wait_recv(gq_ref.at[:, pl.ds(h * width, width)], br.at[1, h])
        wait_recv(kv_in.at[h], br.at[0, h])

    @pl.when(last_x)
    def _():
        for h in range(KVH):
            wait_recv(prior_in.at[h], pr.at[h])
        results(True)

    @pl.when(jnp.logical_not(last_x))
    def _():
        results(False)

    for copy, condition in sent:
        if condition is None:
            copy.wait_send()
        else:
            @pl.when(condition)
            def _(copy=copy):
                copy.wait_send()


def on_device(queries, keys, values, grad_out, positions):
    ny, nzh = lax.axis_size("inner"), lax.axis_size("outer") // NX
    rows, width = queries.shape
    group = width // (KVH * D)
    half = ny // 2
    lanes = group * D
    anywhere = pl.BlockSpec(memory_space=pl.ANY)
    vmem = pl.BlockSpec(memory_space=pltpu.VMEM)
    dma = pltpu.SemaphoreType.DMA
    return pl.pallas_call(
        functools.partial(kernel, ny, nzh, group),
        out_shape=tuple(jax.ShapeDtypeStruct(a.shape, BF16) for a in (queries, keys, values)),
        in_specs=[anywhere] * 4 + [vmem],
        out_specs=(anywhere, vmem, vmem),
        scratch_shapes=[
            pltpu.VMEM((32, KVH * D), BF16),
            pltpu.VMEM((32, KVH * D), BF16),
            pltpu.VMEM((KVH, 64, D), BF16),
            pltpu.VMEM((16, 128), BF16),
            pltpu.VMEM((ny, 3, 272, D), BF16),
            pltpu.VMEM((2, 128, lanes), BF16),
            pltpu.VMEM((2, 128, lanes), BF16),
            pltpu.VMEM((2, lanes, D), BF16),
            pltpu.VMEM((2, lanes, D), BF16),
            pltpu.VMEM((2, D, lanes), BF16),
            pltpu.VMEM((2, D, lanes), BF16),
            pltpu.VMEM((ny, 2, 256, lanes), BF16),
            pltpu.VMEM((ny, 2, 256, lanes), F32),
            pltpu.VMEM((ny, 2, 1, lanes), F32),
            pltpu.VMEM((2, 1, lanes), F32),
            pltpu.VMEM((2, 8, lanes), F32),
            pltpu.VMEM((2, 8, lanes), F32),
            pltpu.VMEM((2, D, lanes), F32),
            pltpu.VMEM((ny, 2, 2, 256, D), F32),
            pltpu.VMEM((2, half, 3, 2, 128, D), BF16),
            pltpu.VMEM((2, half, 3, 2, 128, D), BF16),
            pltpu.VMEM((ny, 2, 128, D), BF16),
            pltpu.VMEM((ny, 2, 128, D), BF16),
            pltpu.VMEM((3, 4, 64, D), BF16),
            pltpu.VMEM((KVH, 64, D), BF16),
            pltpu.VMEM((KVH, 64, D), BF16),
            pltpu.VMEM((2, 128, lanes), BF16),
            dma((2,)),
            dma((4, 8)), dma((4, 8)),
            dma((8,)), dma((4,)),
            dma((2, half + 1)),
            dma((2, half, 3)), dma((2, half, 3)),
            dma((2, half, 3)), dma((2, half, 3)),
            dma((half + 1, 2)), dma((half + 1, 2)),
            dma((2, 8)), dma((2, 8)),
            dma((4,)), dma((8,)),
        ],
        compiler_params=pltpu.CompilerParams(
            collective_id=0, has_side_effects=True, vmem_limit_bytes=56 * 1024 * 1024
        ),
        name="banded_backward",
    )(queries, keys, values, grad_out, positions.reshape(1, -1))


def solution(mesh):
    tokens = P(("outer", "inner", "head"), None)
    return jax.shard_map(
        on_device,
        mesh=mesh,
        in_specs=(tokens, tokens, tokens, tokens, P(("outer", "inner"))),
        out_specs=(tokens, tokens, tokens),
        check_vma=False,
    )
```

```python
import functools

import jax
import jax.numpy as jnp
from jax import lax
from jax.experimental import pallas as pl
from jax.experimental.pallas import tpu as pltpu
from jax.sharding import PartitionSpec as P

D = 128
RUN = 64
NX = 4
KVH = 8
MESH = pl.DeviceIdType.MESH
NEG = -1e30
SCALE = D ** -0.5
EXP_SCALE = SCALE * 1.4426950408889634
F32 = jnp.float32
BF16 = jnp.bfloat16


def dot(a, b):
    return lax.dot_general(a, b, (((1,), (0,)), ((), ())), preferred_element_type=F32)


def sum8(value):
    rows, width = value.shape
    return jnp.sum(value.reshape(rows // 8, 8, width), axis=0)


def kernel(
    ny, nzh, group,
    q_ref, k_ref, v_ref, go_ref, pos_ref,
    gq_ref, gk_ref, gv_ref,
    kst, vst, staged, poss, kv, qbuf, gbuf, qrow, grow, q_t, g_t, pst, dpst, mst, mrun, lrun, drun, dq_t,
    acc, part, rbuf, sib_out, sib_in, kv_out, kv_in, prior_in, gq_out,
    ls, fs, fr, os, orr, ks, hs, hr, rs, rr, ss, sr, bs, br, ps, pr, ready,
):
    half = ny // 2
    width = group * D
    hd, y, o = lax.axis_index("head"), lax.axis_index("inner"), lax.axis_index("outer")
    zl, c = lax.div(hd, 2), lax.rem(hd, 2)
    zh, x = lax.div(o, NX), lax.rem(o, NX)
    xc, s = lax.div(x, 2), lax.rem(x, 2)
    kvh = zl * NX + x
    own = c == xc
    core0, core1 = c == 0, c == 1
    first = jnp.logical_and(core0, zh == 0)
    has_prior = jnp.logical_and(core0, zh > 0)
    gives_prior = jnp.logical_and(core1, zh < nzh - 1)
    owns_prior = jnp.logical_and(x == NX - 1, zh < nzh - 1)

    forward = []
    for a in range(2):
        for b in range(NX):
            zl2, x2 = lax.rem(zl + a, 2), lax.rem(x + b, NX)
            forward.append(((zl2 * 2 + xc, y, zh * NX + x2), zl2 * NX + x2, x2, own if a + b == 0 else None))
    back = []
    for i in range(4):
        for s2 in range(2):
            hd2 = lax.rem(hd + i, 4)
            me = (2 * c + s2 == x) if i == 0 else None
            back.append(((hd2, y, zh * NX + 2 * c + s2), hd2, s2, me))
    zh_after, zh_before = jnp.minimum(zh + 1, nzh - 1), jnp.maximum(zh - 1, 0)
    sibling = (hd + 1 - 2 * c, y, o)
    heir, donor = (sibling[0], y, zh_after * NX + x), (sibling[0], y, zh_before * NX + x)
    owners = [((hd2, y, zh_before * NX + NX - 1), hd2) for hd2 in range(4)]
    ring = ((hd, lax.rem(y + 1, ny), o), (hd, lax.rem(y + ny - 1, ny), o))
    ring2 = ((hd, lax.rem(y + 2, ny), o), (hd, lax.rem(y + ny - 2, ny), o))

    def remote(src, dst, send, recv, device):
        return pltpu.make_async_remote_copy(
            src_ref=src, dst_ref=dst, send_sem=send, recv_sem=recv, device_id=device, device_id_type=MESH
        )

    def wait_recv(dst, recv):
        remote(dst, dst, recv, recv, ring[0]).wait_recv()

    sent = []

    def send(src, dst, send_sem, recv_sem, device, me=None):
        copy = remote(src, dst, send_sem, recv_sem, device)
        if me is None:
            copy.start()
            sent.append((copy, None))
        else:
            @pl.when(me)
            def _():
                pltpu.make_async_copy(src, dst, recv_sem).start()

            away = jnp.logical_not(me)

            @pl.when(away)
            def _():
                copy.start()

            sent.append((copy, away))

    def send_if(condition, *copies):
        copies = [remote(*copy) for copy in copies]

        @pl.when(condition)
        def _():
            for copy in copies:
                copy.start()

        sent.extend((copy, condition) for copy in copies)

    barrier = pltpu.get_barrier_semaphore()

    def greet(device):
        pl.semaphore_signal(barrier, inc=1, device_id=device, device_id_type=MESH)

    @pl.when(has_prior)
    def _():
        greet(donor)

    for device, _, _, me in back:
        if me is None:
            greet(device)
        else:
            @pl.when(jnp.logical_not(me))
            def _(device=device):
                greet(device)
    for device in ring + ring2:
        greet(device)

    @pl.when(jnp.logical_not(own))
    def _():
        greet(sibling)

    @pl.when(owns_prior)
    def _():
        for zl2 in range(2):
            for x2 in range(NX):
                greet((2 * zl2, y, zh_after * NX + x2))


    loads = [pltpu.make_async_copy(src, dst, ls.at[i]) for i, (src, dst) in enumerate(((k_ref, kst), (v_ref, vst)))]
    for load in loads:
        load.start()
    run_id = lax.rem(lax.div(pos_ref[...], RUN), 2 * ny).astype(F32)
    poss[...] = jnp.broadcast_to(run_id, poss.shape).astype(BF16)
    for load in loads:
        load.wait()
    for h in range(KVH):
        staged[h, :32, :] = kst[:, h * D:(h + 1) * D]
        staged[h, 32:, :] = vst[:, h * D:(h + 1) * D]
    @pl.when(first)
    def _():
        for origin in range(ny):
            kv[origin, 0] = jnp.zeros(kv.shape[2:], BF16)

    mrun[...] = jnp.full(mrun.shape, NEG, F32)
    lrun[...] = jnp.zeros(lrun.shape, F32)
    drun[...] = jnp.zeros(drun.shape, F32)
    dq_t[...] = jnp.zeros(dq_t.shape, F32)
    pl.semaphore_wait(
        barrier,
        12 + gives_prior.astype(jnp.int32) + 4 * has_prior.astype(jnp.int32),
    )

    kv_rows = pl.ds(pl.multiple_of(hd * 64, 64), 64)
    for n, (device, kvh2, x2, me) in enumerate(forward):
        send(staged.at[kvh2], kv.at[y, 1 + s, kv_rows, :], fs.at[0, n], fr.at[0, s * 4 + hd], device, me)
    for n, (device, kvh2, x2, me) in enumerate(forward):
        runs = (poss, kv.at[y, 1 + s, pl.ds(256, 16), :], fs.at[3, n], fr.at[3, s], device)
        mine = x2 == hd
        if me is None:
            send_if(mine, runs)
        else:
            @pl.when(jnp.logical_and(mine, me))
            def _(runs=runs):
                pltpu.make_async_copy(runs[0], runs[1], runs[3]).start()

            send_if(jnp.logical_and(mine, jnp.logical_not(me)), runs)

    def view(origin, p, d, way):
        rows = pl.ds(0, 272 if p else 256)
        if d == half:
            rows = pl.ds(0, 128) if way == 0 else pl.ds(128, 144 if p else 128)
        return kv.at[origin, p, rows, :]

    def origin_at(way, d):
        return lax.rem(y + ny + (-d if way == 0 else d), ny)

    def gather_send(way, d, p, far=1):
        piece = view(origin_at(way, d - far), p, d, way)
        copy = (piece, piece, hs.at[way, d - 1, p], hr.at[way, d - 1, p], (ring, ring2)[far - 1][way])
        if p == 0:
            send_if(has_prior, copy)
        else:
            send(*copy)

    def hand_over(way, d):
        origin = origin_at(way, d)
        rows = pl.ds(0, 256) if d < half else pl.ds(128 * way, 128)
        send_if(core0, (
            kv.at[origin, 2, rows, :], kv.at[origin, 0, rows, :], ks.at[way, d - 1], hr.at[way, d - 1, 0],
            sibling,
        ))

    def gather_events(d):
        def event(way, p):
            piece = view(origin_at(way, d), p, d, way)
            if p == 0:
                @pl.when(jnp.logical_not(first))
                def _():
                    wait_recv(piece, hr.at[way, d - 1, p])
            else:
                wait_recv(piece, hr.at[way, d - 1, p])
            if p and d < half:
                gather_send(way, d + 1, p)
            if p == 0 and d % 2 == 0:
                for far in (1, 2):
                    if d + far <= half:
                        gather_send(way, d + far, 0, far)
            if p == 2:
                hand_over(way, d)

        return [functools.partial(event, way, p) for p in (2, 1, 0) for way in range(2)]

    for p in (2, 1):
        for hd2 in range(4):
            wait_recv(kv.at[y, p, pl.ds(hd2 * 64, 64), :], fr.at[0, (p - 1) * 4 + hd2])
        wait_recv(kv.at[y, p, pl.ds(256, 16), :], fr.at[3, p - 1])
        for way in range(2):
            gather_send(way, 1, p)
        if p == 2:
            block, prior = (kv.at[y, i, pl.ds(0, 256), :] for i in (2, 0))
            send_if(gives_prior, (block, prior, os, orr, heir))
            send_if(core0, (block, prior, os, orr, sibling))
    token_rows = pl.ds(pl.multiple_of(hd * 32, 32), 32)
    for n, (device, kvh2, x2, me) in enumerate(forward):
        q_cols = pl.ds(pl.multiple_of(kvh2 * width, D), width)
        send(q_ref.at[:, q_cols], qbuf.at[s, token_rows, :], fs.at[1, n], fr.at[1, s * 4 + hd], device, me)
        send(go_ref.at[:, q_cols], gbuf.at[s, token_rows, :], fs.at[2, n], fr.at[2, s * 4 + hd], device, me)


    for device, kvh2, x2, me in forward:
        if me is None:
            pl.semaphore_signal(ready, inc=1, device_id=device, device_id_type=MESH)
        else:
            @pl.when(jnp.logical_not(me))
            def _(device=device):
                pl.semaphore_signal(ready, inc=1, device_id=device, device_id_type=MESH)

    @pl.when(jnp.logical_not(first))
    def _():
        wait_recv(kv.at[y, 0, pl.ds(0, 256), :], orr)

    for far in (1, 2):
        for way in range(2):
            gather_send(way, far, 0, far)
    for d in range(1, half - 1):
        for event in gather_events(d):
            event()

    for s2 in range(2):
        for hd2 in range(4):
            wait_recv(qbuf.at[s2, pl.ds(hd2 * 32, 32), :], fr.at[1, s2 * 4 + hd2])
            wait_recv(gbuf.at[s2, pl.ds(hd2 * 32, 32), :], fr.at[2, s2 * 4 + hd2])
        for g in range(group):
            cols = slice(g * D, (g + 1) * D)
            for src, rows_ref, t_ref in ((qbuf, qrow, q_t), (gbuf, grow, g_t)):
                piece = src[s2, :, cols]
                rows_ref[s2, cols, :] = piece
                t_ref[s2, :, cols] = piece.T

    key_off = lax.rem(lax.broadcasted_iota(jnp.int32, (128, 128), 0), RUN).astype(F32)
    row_off = lax.rem(lax.broadcasted_iota(jnp.int32, (8, 128), 1), RUN).astype(F32)

    def rows_of(origin, qb, which):
        at = [pl.ds(hd2 * 64 + which * 32, 32) for hd2 in range(4)]
        return jnp.concatenate([kv[origin, qb + p, rows, :] for p in range(2) for rows in at], axis=0)

    def forward_chunk(origin):
        def block(qb, _):
            scores = dot(rows_of(origin, qb, 0), q_t[qb])
            dprobs = dot(rows_of(origin, qb, 1), g_t[qb])
            dpst[origin, qb] = dprobs
            runs = kv[origin, qb + 1, pl.ds(256, 16), :].astype(F32)[:1, :]
            key_pos = jnp.broadcast_to(runs, (128, 128)).T * RUN + key_off
            row_runs = kv[y, qb + 1, pl.ds(256, 16), :].astype(F32)[:1, :]
            allowed = key_pos <= row_runs * RUN + row_off[:1, :]
            penalty = jnp.where(jnp.logical_and(first, qb == 0), -NEG, 0.0)
            prior = scores[:128]
            near = jnp.concatenate(
                [jnp.where(allowed, scores[128:, g * D:(g + 1) * D], NEG) for g in range(group)], axis=1
            )
            prior_top = jnp.max(prior, axis=0, keepdims=True) - penalty
            old = mrun[qb]
            top = jnp.maximum(old, jnp.maximum(prior_top, jnp.max(near, axis=0, keepdims=True)))
            mrun[qb] = top
            mst[origin, qb] = top
            shift = top * EXP_SCALE
            probs = jnp.concatenate(
                [jnp.exp2(prior * EXP_SCALE - (shift + penalty)), jnp.exp2(near * EXP_SCALE - shift)], axis=0
            )
            faded = jnp.exp2((old - top) * EXP_SCALE)
            lrun[qb] = lrun[qb] * faded + sum8(probs)
            drun[qb] = drun[qb] * faded + sum8(probs * dprobs)
            pst[origin, qb] = probs.astype(BF16)
            return 0

        lax.fori_loop(0, 2, block, 0)

    def chunk_at(d, j):
        return lax.rem(y + ny + (1 - 2 * j) * d, ny)

    chunks = [(0, 0)] + [(d, j) for d in range(1, half - 1) for j in range(2)]
    events = gather_events(half - 1)
    for i, event in enumerate(events):
        event()
        for d, j in chunks[i * len(chunks) // len(events):(i + 1) * len(chunks) // len(events)]:
            forward_chunk(chunk_at(d, j))
    for j in range(2):
        forward_chunk(chunk_at(half - 1, j))
    for event in gather_events(half):
        event()
    forward_chunk(chunk_at(half, 0))

    for qb in range(2):
        inverse = 1.0 / jnp.sum(lrun[qb], axis=0, keepdims=True)
        delta = jnp.sum(drun[qb], axis=0, keepdims=True) * inverse
        lrun[qb] = jnp.broadcast_to(inverse, lrun.shape[1:])
        drun[qb] = jnp.broadcast_to(delta, drun.shape[1:])

    def backward_chunk(d, j):
        origin = chunk_at(d, j)

        def block(qb, _):
            weight = jnp.exp2((mst[origin, qb] - mrun[qb]) * EXP_SCALE) * lrun[qb, :1, :]
            probs = pst[origin, qb].astype(F32) * weight
            dscores = (probs * (dpst[origin, qb] - drun[qb, :1, :])).astype(BF16)
            acc[origin, qb, 0] = dot(dscores, qrow[qb]) * SCALE
            acc[origin, qb, 1] = dot(probs.astype(BF16), grow[qb])
            dq_t[qb] += dot(rows_of(origin, qb, 0).T, dscores)
            return 0

        lax.fori_loop(0, 2, block, 0)

        @pl.when(core1)
        def _():
            sib_out[origin] = acc[origin, 0, :, :128, :].astype(BF16)

        send_if(core1, (sib_out.at[origin], sib_in.at[origin], ss.at[d, j], sr.at[d, j], sibling))

    def term(d, j, p, which):
        origin = chunk_at(d, j)
        if p == 0:
            return acc[origin, 0, which, :128, :]
        if p == 1:
            return acc[origin, 0, which, 128:, :] + acc[origin, 1, which, :128, :]
        mine = acc[origin, 1, which, 128:, :]
        return mine + jnp.where(core0, sib_in[origin, which].astype(F32), 0.0)

    def from_sibling(d, j):
        @pl.when(core0)
        def _():
            wait_recv(sib_in.at[chunk_at(d, j)], sr.at[d, j])

    def scatter(n, way, p):
        d = half - n
        if n == 1:
            wait_recv(rbuf.at[way, 0, p, way], rr.at[way, 0, p])
        elif n > 1:
            wait_recv(rbuf.at[way, n - 1, p], rr.at[way, n - 1, p])
        for which in range(2):
            if n == 0 and which != way:
                continue
            total = term(d, way if n else 0, p, which)
            if n > 1 or n == 1 and which == way:
                total = total + rbuf[way, n - 1, p, which].astype(F32)
            part[way, n, p, which] = total.astype(BF16)

    def scatter_events(n):
        def event(way, p):
            if p == 2 and (n or not way):
                from_sibling(half - n, way)
            at = (way, n, p) if n else (way, n, p, way)
            copy = (part.at[at], rbuf.at[at], rs.at[way, n, p], rr.at[way, n, p], ring[way])
            if p == 0:
                @pl.when(has_prior)
                def _():
                    scatter(n, way, p)

                send_if(has_prior, copy)
            else:
                scatter(n, way, p)
                send(*copy)

        return [functools.partial(event, way, p) for p in range(3) for way in range(2)]

    backward_chunk(half, 0)
    for event in scatter_events(0):
        event()
    for n in range(1, half):
        for d in (half - 1, half - 2) if n == 1 else (half - n - 1,):
            for j in range(2 if d else 1):
                backward_chunk(d, j)
        if n == half - 1:
            for s2 in range(2):
                for g in range(group):
                    cols = slice(g * D, (g + 1) * D)
                    gq_out[s2, :, cols] = (dq_t[s2, :, cols].T * SCALE).astype(BF16)
            pl.semaphore_wait(ready, 8 - own.astype(jnp.int32))
            q_cols = pl.ds(pl.multiple_of(kvh * width, D), width)
            for m, (device, hd2, s2, me) in enumerate(back):
                rows = pl.ds(pl.multiple_of(hd2 * 32, 32), 32)
                send(gq_out.at[s2, rows, :], gq_ref.at[:, q_cols], bs.at[1, m], br.at[1, kvh], device, me)
        for event in scatter_events(n):
            event()

    def finish(p):
        for way in range(2):
            wait_recv(rbuf.at[way, half - 1, p], rr.at[way, half - 1, p])
        for which in range(2):
            total = term(0, 0, p, which)
            total = total + rbuf[0, half - 1, p, which].astype(F32) + rbuf[1, half - 1, p, which].astype(F32)
            for hd2 in range(4):
                kv_out[p, hd2, pl.ds(which * 32, 32), :] = total[hd2 * 32:(hd2 + 1) * 32].astype(BF16)

    @pl.when(has_prior)
    def _():
        finish(0)

    send_if(has_prior, *(
        (kv_out.at[0, hd2], prior_in.at[kvh], ps.at[hd2], pr.at[kvh], device) for device, hd2 in owners
    ))
    for p in (1, 2):
        if p == 2:
            from_sibling(0, 0)
        finish(p)
        for m, (device, hd2, s2, me) in enumerate(back):
            if s2 == p - 1:
                send(kv_out.at[p, hd2], kv_in.at[kvh], bs.at[0, m], br.at[0, kvh], device, me)

    def results(with_prior):
        for h in range(KVH):
            both = kv_in[h]
            if with_prior:
                both = (both.astype(F32) + prior_in[h].astype(F32)).astype(BF16)
            cols = slice(h * D, (h + 1) * D)
            gk_ref[:, cols] = both[:32]
            gv_ref[:, cols] = both[32:]

    for h in range(KVH):
        wait_recv(gq_ref.at[:, pl.ds(h * width, width)], br.at[1, h])
        wait_recv(kv_in.at[h], br.at[0, h])

    @pl.when(owns_prior)
    def _():
        for h in range(KVH):
            wait_recv(prior_in.at[h], pr.at[h])
        results(True)

    @pl.when(jnp.logical_not(owns_prior))
    def _():
        results(False)

    for copy, condition in sent:
        if condition is None:
            copy.wait_send()
        else:
            @pl.when(condition)
            def _(copy=copy):
                copy.wait_send()


def on_device(queries, keys, values, grad_out, positions):
    ny, nzh = lax.axis_size("inner"), lax.axis_size("outer") // NX
    rows, width = queries.shape
    group = width // (KVH * D)
    half = ny // 2
    lanes = group * D
    anywhere = pl.BlockSpec(memory_space=pl.ANY)
    vmem = pl.BlockSpec(memory_space=pltpu.VMEM)
    dma = pltpu.SemaphoreType.DMA
    return pl.pallas_call(
        functools.partial(kernel, ny, nzh, group),
        out_shape=tuple(jax.ShapeDtypeStruct(a.shape, BF16) for a in (queries, keys, values)),
        in_specs=[anywhere] * 4 + [vmem],
        out_specs=(anywhere, vmem, vmem),
        scratch_shapes=[
            pltpu.VMEM((32, KVH * D), BF16),
            pltpu.VMEM((32, KVH * D), BF16),
            pltpu.VMEM((KVH, 64, D), BF16),
            pltpu.VMEM((16, 128), BF16),
            pltpu.VMEM((ny, 3, 272, D), BF16),
            pltpu.VMEM((2, 128, lanes), BF16),
            pltpu.VMEM((2, 128, lanes), BF16),
            pltpu.VMEM((2, lanes, D), BF16),
            pltpu.VMEM((2, lanes, D), BF16),
            pltpu.VMEM((2, D, lanes), BF16),
            pltpu.VMEM((2, D, lanes), BF16),
            pltpu.VMEM((ny, 2, 256, lanes), BF16),
            pltpu.VMEM((ny, 2, 256, lanes), F32),
            pltpu.VMEM((ny, 2, 1, lanes), F32),
            pltpu.VMEM((2, 1, lanes), F32),
            pltpu.VMEM((2, 8, lanes), F32),
            pltpu.VMEM((2, 8, lanes), F32),
            pltpu.VMEM((2, D, lanes), F32),
            pltpu.VMEM((ny, 2, 2, 256, D), F32),
            pltpu.VMEM((2, half, 3, 2, 128, D), BF16),
            pltpu.VMEM((2, half, 3, 2, 128, D), BF16),
            pltpu.VMEM((ny, 2, 128, D), BF16),
            pltpu.VMEM((ny, 2, 128, D), BF16),
            pltpu.VMEM((3, 4, 64, D), BF16),
            pltpu.VMEM((KVH, 64, D), BF16),
            pltpu.VMEM((KVH, 64, D), BF16),
            pltpu.VMEM((2, 128, lanes), BF16),
            dma((2,)),
            dma((4, 8)), dma((4, 8)),
            dma, dma,
            dma((2, half)),
            dma((2, half, 3)), dma((2, half, 3)),
            dma((2, half, 3)), dma((2, half, 3)),
            dma((half + 1, 2)), dma((half + 1, 2)),
            dma((2, 8)), dma((2, 8)),
            dma((4,)), dma((8,)),
            pltpu.SemaphoreType.REGULAR,
        ],
        compiler_params=pltpu.CompilerParams(
            collective_id=0, has_side_effects=True, vmem_limit_bytes=56 * 1024 * 1024
        ),
        name="banded_backward",
    )(queries, keys, values, grad_out, positions.reshape(1, -1))


def solution(mesh):
    tokens = P(("outer", "inner", "head"), None)
    return jax.shard_map(
        on_device,
        mesh=mesh,
        in_specs=(tokens, tokens, tokens, tokens, P(("outer", "inner"))),
        out_specs=(tokens, tokens, tokens),
        check_vma=False,
    )
```

```python
import functools

import jax
import jax.numpy as jnp
from jax import lax
from jax.experimental import pallas as pl
from jax.experimental.pallas import tpu as pltpu
from jax.sharding import PartitionSpec as P

D = 128
RUN = 64
NX = 4
KVH = 8
MESH = pl.DeviceIdType.MESH
TILE = 256
NEG = -1e30
SCALE = D ** -0.5
EXP_SCALE = SCALE * 1.4426950408889634
F32 = jnp.float32
BF16 = jnp.bfloat16


def dot(a, b):
    return lax.dot_general(a, b, (((1,), (0,)), ((), ())), preferred_element_type=F32)


def sum8(value):
    rows, width = value.shape
    return jnp.sum(value.reshape(rows // 8, 8, width), axis=0)


def kernel(
    ny, nzh, group,
    q_ref, k_ref, v_ref, go_ref, pos_ref,
    gq_ref, gk_ref, gv_ref,
    kst, vst, staged, poss, kv, qbuf, gbuf, qrow, grow, q_t, g_t, pst, mst, mrun, lrun, drun, dq_t,
    acc, part, rbuf, sib_out, sib_in, kv_out, kv_in, prior_in, gq_out,
    ls, fs, fr, os, orr, ks, hs, hr, rs, rr, ss, sr, bs, br, ps, pr, ready,
):
    half = ny // 2
    width = group * D
    hd, y, o = lax.axis_index("head"), lax.axis_index("inner"), lax.axis_index("outer")
    zl, c = lax.div(hd, 2), lax.rem(hd, 2)
    zh, x = lax.div(o, NX), lax.rem(o, NX)
    xc, s = lax.div(x, 2), lax.rem(x, 2)
    kvh = zl * NX + x
    own = c == xc
    core0, core1 = c == 0, c == 1
    first = jnp.logical_and(core0, zh == 0)
    has_prior = jnp.logical_and(core0, zh > 0)
    gives_prior = jnp.logical_and(core1, zh < nzh - 1)
    owns_prior = jnp.logical_and(x == NX - 1, zh < nzh - 1)

    forward = []
    for a in range(2):
        for b in range(NX):
            zl2, x2 = lax.rem(zl + a, 2), lax.rem(x + b, NX)
            forward.append(((zl2 * 2 + xc, y, zh * NX + x2), zl2 * NX + x2, x2, own if a + b == 0 else None))
    back = []
    for i in range(4):
        for s2 in range(2):
            hd2 = lax.rem(hd + i, 4)
            me = (2 * c + s2 == x) if i == 0 else None
            back.append(((hd2, y, zh * NX + 2 * c + s2), hd2, s2, me))
    zh_after, zh_before = jnp.minimum(zh + 1, nzh - 1), jnp.maximum(zh - 1, 0)
    sibling = (hd + 1 - 2 * c, y, o)
    heir, donor = (sibling[0], y, zh_after * NX + x), (sibling[0], y, zh_before * NX + x)
    owners = [((hd2, y, zh_before * NX + NX - 1), hd2) for hd2 in range(4)]
    ring = ((hd, lax.rem(y + 1, ny), o), (hd, lax.rem(y + ny - 1, ny), o))
    ring2 = ((hd, lax.rem(y + 2, ny), o), (hd, lax.rem(y + ny - 2, ny), o))

    def remote(src, dst, send, recv, device):
        return pltpu.make_async_remote_copy(
            src_ref=src, dst_ref=dst, send_sem=send, recv_sem=recv, device_id=device, device_id_type=MESH
        )

    def wait_recv(dst, recv):
        remote(dst, dst, recv, recv, ring[0]).wait_recv()

    sent = []

    def send(src, dst, send_sem, recv_sem, device, me=None):
        copy = remote(src, dst, send_sem, recv_sem, device)
        if me is None:
            copy.start()
            sent.append((copy, None))
        else:
            @pl.when(me)
            def _():
                pltpu.make_async_copy(src, dst, recv_sem).start()

            away = jnp.logical_not(me)

            @pl.when(away)
            def _():
                copy.start()

            sent.append((copy, away))

    def send_if(condition, *copies):
        copies = [remote(*copy) for copy in copies]

        @pl.when(condition)
        def _():
            for copy in copies:
                copy.start()

        sent.extend((copy, condition) for copy in copies)

    barrier = pltpu.get_barrier_semaphore()

    def greet(device):
        pl.semaphore_signal(barrier, inc=1, device_id=device, device_id_type=MESH)

    @pl.when(has_prior)
    def _():
        greet(donor)

    for device, _, _, me in back:
        if me is None:
            greet(device)
        else:
            @pl.when(jnp.logical_not(me))
            def _(device=device):
                greet(device)
    for device in ring + ring2:
        greet(device)

    @pl.when(jnp.logical_not(own))
    def _():
        greet(sibling)

    @pl.when(owns_prior)
    def _():
        for zl2 in range(2):
            for x2 in range(NX):
                greet((2 * zl2, y, zh_after * NX + x2))


    loads = [pltpu.make_async_copy(src, dst, ls.at[i]) for i, (src, dst) in enumerate(((k_ref, kst), (v_ref, vst)))]
    for load in loads:
        load.start()
    run_id = lax.rem(lax.div(pos_ref[...], RUN), 2 * ny).astype(F32)
    poss[...] = jnp.broadcast_to(run_id, poss.shape).astype(BF16)
    for load in loads:
        load.wait()
    for h in range(KVH):
        staged[h, :32, :] = kst[:, h * D:(h + 1) * D]
        staged[h, 32:, :] = vst[:, h * D:(h + 1) * D]
    @pl.when(first)
    def _():
        for origin in range(ny):
            kv[origin, 0] = jnp.zeros(kv.shape[2:], BF16)

    mrun[...] = jnp.full(mrun.shape, NEG, F32)
    lrun[...] = jnp.zeros(lrun.shape, F32)
    drun[...] = jnp.zeros(drun.shape, F32)
    dq_t[...] = jnp.zeros(dq_t.shape, F32)
    pl.semaphore_wait(
        barrier,
        12 + gives_prior.astype(jnp.int32) + 4 * has_prior.astype(jnp.int32),
    )

    kv_rows = pl.ds(pl.multiple_of(hd * 64, 64), 64)
    for n, (device, kvh2, x2, me) in enumerate(forward):
        send(staged.at[kvh2], kv.at[y, 1 + s, kv_rows, :], fs.at[0, n], fr.at[0, s * 4 + hd], device, me)
    for n, (device, kvh2, x2, me) in enumerate(forward):
        runs = (poss, kv.at[y, 1 + s, pl.ds(256, 16), :], fs.at[3, n], fr.at[3, s], device)
        mine = x2 == hd
        if me is None:
            send_if(mine, runs)
        else:
            @pl.when(jnp.logical_and(mine, me))
            def _(runs=runs):
                pltpu.make_async_copy(runs[0], runs[1], runs[3]).start()

            send_if(jnp.logical_and(mine, jnp.logical_not(me)), runs)

    def view(origin, p, d, way):
        rows = pl.ds(0, 272 if p else 256)
        if d == half:
            rows = pl.ds(0, 128) if way == 0 else pl.ds(128, 144 if p else 128)
        return kv.at[origin, p, rows, :]

    def origin_at(way, d):
        return lax.rem(y + ny + (-d if way == 0 else d), ny)

    def gather_send(way, d, p, far=1):
        piece = view(origin_at(way, d - far), p, d, way)
        copy = (piece, piece, hs.at[way, d - 1, p], hr.at[way, d - 1, p], (ring, ring2)[far - 1][way])
        if p == 0:
            send_if(has_prior, copy)
        else:
            send(*copy)

    def hand_over(way, d):
        origin = origin_at(way, d)
        rows = pl.ds(0, 256) if d < half else pl.ds(128 * way, 128)
        send_if(core0, (
            kv.at[origin, 2, rows, :], kv.at[origin, 0, rows, :], ks.at[way, d - 1], hr.at[way, d - 1, 0],
            sibling,
        ))

    def gather_events(d):
        def event(way, p):
            piece = view(origin_at(way, d), p, d, way)
            if p == 0:
                @pl.when(jnp.logical_not(first))
                def _():
                    wait_recv(piece, hr.at[way, d - 1, p])
            else:
                wait_recv(piece, hr.at[way, d - 1, p])
            if p and d < half:
                gather_send(way, d + 1, p)
            if p == 0 and d % 2 == 0:
                for far in (1, 2):
                    if d + far <= half:
                        gather_send(way, d + far, 0, far)
            if p == 2:
                hand_over(way, d)

        return [functools.partial(event, way, p) for p in (2, 1, 0) for way in range(2)]

    for p in (2, 1):
        for hd2 in range(4):
            wait_recv(kv.at[y, p, pl.ds(hd2 * 64, 64), :], fr.at[0, (p - 1) * 4 + hd2])
        wait_recv(kv.at[y, p, pl.ds(256, 16), :], fr.at[3, p - 1])
        for way in range(2):
            gather_send(way, 1, p)
        if p == 2:
            block, prior = (kv.at[y, i, pl.ds(0, 256), :] for i in (2, 0))
            send_if(gives_prior, (block, prior, os, orr, heir))
            send_if(core0, (block, prior, os, orr, sibling))
    token_rows = pl.ds(pl.multiple_of(hd * 32, 32), 32)
    for n, (device, kvh2, x2, me) in enumerate(forward):
        q_cols = pl.ds(pl.multiple_of(kvh2 * width, D), width)
        send(q_ref.at[:, q_cols], qbuf.at[s, token_rows, :], fs.at[1, n], fr.at[1, s * 4 + hd], device, me)
        send(go_ref.at[:, q_cols], gbuf.at[s, token_rows, :], fs.at[2, n], fr.at[2, s * 4 + hd], device, me)


    for device, kvh2, x2, me in forward:
        if me is None:
            pl.semaphore_signal(ready, inc=1, device_id=device, device_id_type=MESH)
        else:
            @pl.when(jnp.logical_not(me))
            def _(device=device):
                pl.semaphore_signal(ready, inc=1, device_id=device, device_id_type=MESH)

    @pl.when(jnp.logical_not(first))
    def _():
        wait_recv(kv.at[y, 0, pl.ds(0, 256), :], orr)

    for far in (1, 2):
        for way in range(2):
            gather_send(way, far, 0, far)
    for d in range(1, half - 1):
        for event in gather_events(d):
            event()

    for s2 in range(2):
        for hd2 in range(4):
            wait_recv(qbuf.at[s2, pl.ds(hd2 * 32, 32), :], fr.at[1, s2 * 4 + hd2])
            wait_recv(gbuf.at[s2, pl.ds(hd2 * 32, 32), :], fr.at[2, s2 * 4 + hd2])
        for g in range(group):
            cols = slice(g * D, (g + 1) * D)
            for src, rows_ref, t_ref in ((qbuf, qrow, q_t), (gbuf, grow, g_t)):
                piece = src[s2, :, cols]
                rows_ref[s2, cols, :] = piece
                t_ref[s2, :, cols] = piece.T

    key_off = lax.rem(lax.broadcasted_iota(jnp.int32, (128, 128), 0), RUN).astype(F32)
    row_off = lax.rem(lax.broadcasted_iota(jnp.int32, (8, 128), 1), RUN).astype(F32)

    penalty = jnp.where(first, -NEG, 0.0)

    def rows_of(origin, qb, which):
        at = [pl.ds(hd2 * 64 + which * 32, 32) for hd2 in range(4)]
        return jnp.concatenate([kv[origin, qb + p, rows, :] for p in range(2) for rows in at], axis=0)

    def forward_chunk(origin):
        for qb in range(2):
            keys, vals = rows_of(origin, qb, 0), rows_of(origin, qb, 1)
            runs = kv[origin, qb + 1, pl.ds(256, 16), :].astype(F32)[:1, :]
            key_pos = jnp.broadcast_to(runs, (128, 128)).T * RUN + key_off
            row_runs = kv[y, qb + 1, pl.ds(256, 16), :].astype(F32)[:1, :]
            allowed = key_pos <= row_runs * RUN + row_off[:1, :]
            for tile in range(0, width, TILE):
                cols = slice(tile, tile + TILE)
                scores = dot(keys, q_t[qb, :, cols])
                prior = scores[:128]
                near = jnp.concatenate(
                    [jnp.where(allowed, scores[128:, g:g + D], NEG) for g in range(0, TILE, D)], axis=1
                )
                prior_top = jnp.max(prior, axis=0, keepdims=True)
                if qb == 0:
                    prior_top = prior_top - penalty
                old = mrun[qb, :, cols]
                top = jnp.maximum(old, jnp.maximum(prior_top, jnp.max(near, axis=0, keepdims=True)))
                mrun[qb, :, cols] = top
                mst[origin, qb, :, cols] = top
                shift = top * EXP_SCALE
                prior_shift = shift + penalty if qb == 0 else shift
                probs = jnp.concatenate(
                    [jnp.exp2(prior * EXP_SCALE - prior_shift), jnp.exp2(near * EXP_SCALE - shift)], axis=0
                )
                faded = jnp.exp2((old - top) * EXP_SCALE)
                lrun[qb, :, cols] = lrun[qb, :, cols] * faded + sum8(probs)
                pst[origin, qb, :, cols] = probs.astype(BF16)
                dprobs = dot(vals, g_t[qb, :, cols])
                drun[qb, :, cols] = drun[qb, :, cols] * faded + sum8(probs * dprobs)

    def chunk_at(d, j):
        return lax.rem(y + ny + (1 - 2 * j) * d, ny)

    chunks = [(0, 0)] + [(d, j) for d in range(1, half - 1) for j in range(2)]
    events = gather_events(half - 1)
    for i, event in enumerate(events):
        event()
        for d, j in chunks[i * len(chunks) // len(events):(i + 1) * len(chunks) // len(events)]:
            forward_chunk(chunk_at(d, j))
    for j in range(2):
        forward_chunk(chunk_at(half - 1, j))
    for event in gather_events(half):
        event()
    forward_chunk(chunk_at(half, 0))

    for qb in range(2):
        inverse = 1.0 / jnp.sum(lrun[qb], axis=0, keepdims=True)
        delta = jnp.sum(drun[qb], axis=0, keepdims=True) * inverse
        lrun[qb] = jnp.broadcast_to(inverse, lrun.shape[1:])
        drun[qb] = jnp.broadcast_to(delta, drun.shape[1:])

    def backward_chunk(d, j):
        origin = chunk_at(d, j)

        for qb in range(2):
            keys, vals = rows_of(origin, qb, 0), rows_of(origin, qb, 1)
            probs16, dscores16 = [], []
            for tile in range(0, width, TILE):
                cols = slice(tile, tile + TILE)
                weight = jnp.exp2((mst[origin, qb, :, cols] - mrun[qb, :, cols]) * EXP_SCALE) * lrun[qb, :1, cols]
                probs = pst[origin, qb, :, cols].astype(F32) * weight
                dprobs = dot(vals, g_t[qb, :, cols])
                probs16.append(probs.astype(BF16))
                dscores16.append((probs * (dprobs - drun[qb, :1, cols])).astype(BF16))
            dscores = jnp.concatenate(dscores16, axis=1)
            acc[origin, qb, 1] = dot(jnp.concatenate(probs16, axis=1), grow[qb])
            acc[origin, qb, 0] = dot(dscores, qrow[qb])
            dq_t[qb] += dot(keys.T, dscores)

        @pl.when(core1)
        def _():
            sib_out[origin] = acc[origin, 0, :, :128, :].astype(BF16)

        send_if(core1, (sib_out.at[origin], sib_in.at[origin], ss.at[d, j], sr.at[d, j], sibling))

    def term(d, j, p, which):
        origin = chunk_at(d, j)
        if p == 0:
            return acc[origin, 0, which, :128, :]
        if p == 1:
            return acc[origin, 0, which, 128:, :] + acc[origin, 1, which, :128, :]
        mine = acc[origin, 1, which, 128:, :]
        return mine + jnp.where(core0, sib_in[origin, which].astype(F32), 0.0)

    def from_sibling(d, j):
        @pl.when(core0)
        def _():
            wait_recv(sib_in.at[chunk_at(d, j)], sr.at[d, j])

    def scatter(n, way, p):
        d = half - n
        if n == 1:
            wait_recv(rbuf.at[way, 0, p, way], rr.at[way, 0, p])
        elif n > 1:
            wait_recv(rbuf.at[way, n - 1, p], rr.at[way, n - 1, p])
        for which in range(2):
            if n == 0 and which != way:
                continue
            total = term(d, way if n else 0, p, which)
            if n > 1 or n == 1 and which == way:
                total = total + rbuf[way, n - 1, p, which].astype(F32)
            part[way, n, p, which] = total.astype(BF16)

    def scatter_events(n):
        def event(way, p):
            if p == 2 and (n or not way):
                from_sibling(half - n, way)
            at = (way, n, p) if n else (way, n, p, way)
            copy = (part.at[at], rbuf.at[at], rs.at[way, n, p], rr.at[way, n, p], ring[way])
            if p == 0:
                @pl.when(has_prior)
                def _():
                    scatter(n, way, p)

                send_if(has_prior, copy)
            else:
                scatter(n, way, p)
                send(*copy)

        return [functools.partial(event, way, p) for p in range(3) for way in range(2)]

    backward_chunk(half, 0)
    for event in scatter_events(0):
        event()
    for n in range(1, half):
        for d in (half - 1, half - 2) if n == 1 else (half - n - 1,):
            for j in range(2 if d else 1):
                backward_chunk(d, j)
        if n == half - 1:
            for s2 in range(2):
                for g in range(group):
                    cols = slice(g * D, (g + 1) * D)
                    gq_out[s2, :, cols] = dq_t[s2, :, cols].T.astype(BF16)
            pl.semaphore_wait(ready, 8 - own.astype(jnp.int32))
            q_cols = pl.ds(pl.multiple_of(kvh * width, D), width)
            for m, (device, hd2, s2, me) in enumerate(back):
                rows = pl.ds(pl.multiple_of(hd2 * 32, 32), 32)
                send(gq_out.at[s2, rows, :], gq_ref.at[:, q_cols], bs.at[1, m], br.at[1, kvh], device, me)
        for event in scatter_events(n):
            event()

    def finish(p):
        for way in range(2):
            wait_recv(rbuf.at[way, half - 1, p], rr.at[way, half - 1, p])
        for which in range(2):
            total = term(0, 0, p, which)
            total = total + rbuf[0, half - 1, p, which].astype(F32) + rbuf[1, half - 1, p, which].astype(F32)
            for hd2 in range(4):
                kv_out[p, hd2, pl.ds(which * 32, 32), :] = total[hd2 * 32:(hd2 + 1) * 32].astype(BF16)

    @pl.when(has_prior)
    def _():
        finish(0)

    send_if(has_prior, *(
        (kv_out.at[0, hd2], prior_in.at[kvh], ps.at[hd2], pr.at[kvh], device) for device, hd2 in owners
    ))
    for p in (1, 2):
        if p == 2:
            from_sibling(0, 0)
        finish(p)
        for m, (device, hd2, s2, me) in enumerate(back):
            if s2 == p - 1:
                send(kv_out.at[p, hd2], kv_in.at[kvh], bs.at[0, m], br.at[0, kvh], device, me)

    def results(with_prior):
        for h in range(KVH):
            both = kv_in[h]
            if with_prior:
                both = (both.astype(F32) + prior_in[h].astype(F32)).astype(BF16)
            cols = slice(h * D, (h + 1) * D)
            gk_ref[:, cols] = both[:32]
            gv_ref[:, cols] = both[32:]

    for h in range(KVH):
        wait_recv(gq_ref.at[:, pl.ds(h * width, width)], br.at[1, h])
        wait_recv(kv_in.at[h], br.at[0, h])

    @pl.when(owns_prior)
    def _():
        for h in range(KVH):
            wait_recv(prior_in.at[h], pr.at[h])
        results(True)

    @pl.when(jnp.logical_not(owns_prior))
    def _():
        results(False)

    for copy, condition in sent:
        if condition is None:
            copy.wait_send()
        else:
            @pl.when(condition)
            def _(copy=copy):
                copy.wait_send()


def on_device(queries, keys, values, grad_out, positions):
    ny, nzh = lax.axis_size("inner"), lax.axis_size("outer") // NX
    rows, width = queries.shape
    group = width // (KVH * D)
    half = ny // 2
    lanes = group * D
    anywhere = pl.BlockSpec(memory_space=pl.ANY)
    vmem = pl.BlockSpec(memory_space=pltpu.VMEM)
    dma = pltpu.SemaphoreType.DMA
    grad_query, grad_key, grad_value = pl.pallas_call(
        functools.partial(kernel, ny, nzh, group),
        out_shape=tuple(jax.ShapeDtypeStruct(a.shape, BF16) for a in (queries, keys, values)),
        in_specs=[anywhere] * 4 + [vmem],
        out_specs=(anywhere, vmem, vmem),
        scratch_shapes=[
            pltpu.VMEM((32, KVH * D), BF16),
            pltpu.VMEM((32, KVH * D), BF16),
            pltpu.VMEM((KVH, 64, D), BF16),
            pltpu.VMEM((16, 128), BF16),
            pltpu.VMEM((ny, 3, 272, D), BF16),
            pltpu.VMEM((2, 128, lanes), BF16),
            pltpu.VMEM((2, 128, lanes), BF16),
            pltpu.VMEM((2, lanes, D), BF16),
            pltpu.VMEM((2, lanes, D), BF16),
            pltpu.VMEM((2, D, lanes), BF16),
            pltpu.VMEM((2, D, lanes), BF16),
            pltpu.VMEM((ny, 2, 256, lanes), BF16),
            pltpu.VMEM((ny, 2, 1, lanes), F32),
            pltpu.VMEM((2, 1, lanes), F32),
            pltpu.VMEM((2, 8, lanes), F32),
            pltpu.VMEM((2, 8, lanes), F32),
            pltpu.VMEM((2, D, lanes), F32),
            pltpu.VMEM((ny, 2, 2, 256, D), F32),
            pltpu.VMEM((2, half, 3, 2, 128, D), BF16),
            pltpu.VMEM((2, half, 3, 2, 128, D), BF16),
            pltpu.VMEM((ny, 2, 128, D), BF16),
            pltpu.VMEM((ny, 2, 128, D), BF16),
            pltpu.VMEM((3, 4, 64, D), BF16),
            pltpu.VMEM((KVH, 64, D), BF16),
            pltpu.VMEM((KVH, 64, D), BF16),
            pltpu.VMEM((2, 128, lanes), BF16),
            dma((2,)),
            dma((4, 8)), dma((4, 8)),
            dma, dma,
            dma((2, half)),
            dma((2, half, 3)), dma((2, half, 3)),
            dma((2, half, 3)), dma((2, half, 3)),
            dma((half + 1, 2)), dma((half + 1, 2)),
            dma((2, 8)), dma((2, 8)),
            dma((4,)), dma((8,)),
            pltpu.SemaphoreType.REGULAR,
        ],
        compiler_params=pltpu.CompilerParams(
            collective_id=0, has_side_effects=True, vmem_limit_bytes=56 * 1024 * 1024
        ),
        name="banded_backward",
    )(queries, keys, values, grad_out, positions.reshape(1, -1))
    scaled = [(a.astype(F32) * SCALE).astype(BF16) for a in (grad_query, grad_key)]
    return (*scaled, grad_value)


def solution(mesh):
    tokens = P(("outer", "inner", "head"), None)
    return jax.shard_map(
        on_device,
        mesh=mesh,
        in_specs=(tokens, tokens, tokens, tokens, P(("outer", "inner"))),
        out_specs=(tokens, tokens, tokens),
        check_vma=False,
    )
```

```python
import functools

import jax
import jax.numpy as jnp
from jax import lax
from jax.experimental import pallas as pl
from jax.experimental.pallas import tpu as pltpu
from jax.sharding import PartitionSpec as P

D = 128
RUN = 64
NX = 4
KVH = 8
MESH = pl.DeviceIdType.MESH
TILE = 256
NEG = -1e30
SCALE = D ** -0.5
EXP_SCALE = SCALE * 1.4426950408889634
F32 = jnp.float32
BF16 = jnp.bfloat16


def dot(a, b):
    return lax.dot_general(a, b, (((1,), (0,)), ((), ())), preferred_element_type=F32)


def sum8(value):
    rows, width = value.shape
    return jnp.sum(value.reshape(rows // 8, 8, width), axis=0)


def kernel(
    ny, nzh, group,
    q_ref, k_ref, v_ref, go_ref, pos_ref,
    gq_ref, gk_ref, gv_ref,
    kst, vst, staged, poss, kv, qbuf, gbuf, qrow, grow, q_t, g_t, pst, mst, mrun, lrun, drun, dq_t,
    acc, part, rbuf, sib_out, sib_in, kv_out, kv_in, prior_in, gq_out,
    ls, fs, fr, os, orr, ks, hs, hr, rs, rr, ss, sr, bs, br, ps, pr, ready,
):
    half = ny // 2
    width = group * D
    hd, y, o = lax.axis_index("head"), lax.axis_index("inner"), lax.axis_index("outer")
    zl, c = lax.div(hd, 2), lax.rem(hd, 2)
    zh, x = lax.div(o, NX), lax.rem(o, NX)
    xc, s = lax.div(x, 2), lax.rem(x, 2)
    kvh = zl * NX + x
    own = c == xc
    core0, core1 = c == 0, c == 1
    first = jnp.logical_and(core0, zh == 0)
    has_prior = jnp.logical_and(core0, zh > 0)
    gives_prior = jnp.logical_and(core1, zh < nzh - 1)
    owns_prior = jnp.logical_and(x == NX - 1, zh < nzh - 1)

    forward = []
    for a in range(2):
        for b in range(NX):
            zl2, x2 = lax.rem(zl + a, 2), lax.rem(x + b, NX)
            forward.append(((zl2 * 2 + xc, y, zh * NX + x2), zl2 * NX + x2, x2, own if a + b == 0 else None))
    back = []
    for i in range(4):
        for s2 in range(2):
            hd2 = lax.rem(hd + i, 4)
            me = (2 * c + s2 == x) if i == 0 else None
            back.append(((hd2, y, zh * NX + 2 * c + s2), hd2, s2, me))
    zh_after, zh_before = jnp.minimum(zh + 1, nzh - 1), jnp.maximum(zh - 1, 0)
    sibling = (hd + 1 - 2 * c, y, o)
    heir, donor = (sibling[0], y, zh_after * NX + x), (sibling[0], y, zh_before * NX + x)
    owners = [((hd2, y, zh_before * NX + NX - 1), hd2) for hd2 in range(4)]
    ring = ((hd, lax.rem(y + 1, ny), o), (hd, lax.rem(y + ny - 1, ny), o))
    ring2 = ((hd, lax.rem(y + 2, ny), o), (hd, lax.rem(y + ny - 2, ny), o))

    def remote(src, dst, send, recv, device):
        return pltpu.make_async_remote_copy(
            src_ref=src, dst_ref=dst, send_sem=send, recv_sem=recv, device_id=device, device_id_type=MESH
        )

    def wait_recv(dst, recv):
        remote(dst, dst, recv, recv, ring[0]).wait_recv()

    sent = []

    def send(src, dst, send_sem, recv_sem, device, me=None):
        copy = remote(src, dst, send_sem, recv_sem, device)
        if me is None:
            copy.start()
            sent.append((copy, None))
        else:
            @pl.when(me)
            def _():
                pltpu.make_async_copy(src, dst, recv_sem).start()

            away = jnp.logical_not(me)

            @pl.when(away)
            def _():
                copy.start()

            sent.append((copy, away))

    def send_if(condition, *copies):
        copies = [remote(*copy) for copy in copies]

        @pl.when(condition)
        def _():
            for copy in copies:
                copy.start()

        sent.extend((copy, condition) for copy in copies)

    barrier = pltpu.get_barrier_semaphore()

    def greet(device):
        pl.semaphore_signal(barrier, inc=1, device_id=device, device_id_type=MESH)

    @pl.when(has_prior)
    def _():
        greet(donor)

    for device, _, _, me in back:
        if me is None:
            greet(device)
        else:
            @pl.when(jnp.logical_not(me))
            def _(device=device):
                greet(device)
    for device in ring + ring2:
        greet(device)

    @pl.when(jnp.logical_not(own))
    def _():
        greet(sibling)

    @pl.when(owns_prior)
    def _():
        for zl2 in range(2):
            for x2 in range(NX):
                greet((2 * zl2, y, zh_after * NX + x2))


    loads = [pltpu.make_async_copy(src, dst, ls.at[i]) for i, (src, dst) in enumerate(((k_ref, kst), (v_ref, vst)))]
    for load in loads:
        load.start()
    run_id = lax.rem(lax.div(pos_ref[...], RUN), 2 * ny).astype(F32)
    poss[...] = jnp.broadcast_to(run_id, poss.shape).astype(BF16)
    for load in loads:
        load.wait()
    for h in range(KVH):
        staged[h, :32, :] = kst[:, h * D:(h + 1) * D]
        staged[h, 32:, :] = vst[:, h * D:(h + 1) * D]
    @pl.when(first)
    def _():
        for origin in range(ny):
            kv[origin, 0] = jnp.zeros(kv.shape[2:], BF16)

    mrun[...] = jnp.full(mrun.shape, NEG, F32)
    lrun[...] = jnp.zeros(lrun.shape, F32)
    drun[...] = jnp.zeros(drun.shape, F32)
    dq_t[...] = jnp.zeros(dq_t.shape, F32)
    pl.semaphore_wait(
        barrier,
        12 + gives_prior.astype(jnp.int32) + 4 * has_prior.astype(jnp.int32),
    )

    kv_rows = pl.ds(pl.multiple_of(hd * 64, 64), 64)
    for n, (device, kvh2, x2, me) in enumerate(forward):
        send(staged.at[kvh2], kv.at[y, 1 + s, kv_rows, :], fs.at[0, n], fr.at[0, s * 4 + hd], device, me)
    for n, (device, kvh2, x2, me) in enumerate(forward):
        runs = (poss, kv.at[y, 1 + s, pl.ds(256, 16), :], fs.at[3, n], fr.at[3, s], device)
        mine = x2 == hd
        if me is None:
            send_if(mine, runs)
        else:
            @pl.when(jnp.logical_and(mine, me))
            def _(runs=runs):
                pltpu.make_async_copy(runs[0], runs[1], runs[3]).start()

            send_if(jnp.logical_and(mine, jnp.logical_not(me)), runs)

    def view(origin, p, d, way):
        rows = pl.ds(0, 272 if p else 256)
        if d == half:
            rows = pl.ds(0, 128) if way == 0 else pl.ds(128, 144 if p else 128)
        return kv.at[origin, p, rows, :]

    def origin_at(way, d):
        return lax.rem(y + ny + (-d if way == 0 else d), ny)

    def gather_send(way, d, p, far=1):
        piece = view(origin_at(way, d - far), p, d, way)
        copy = (piece, piece, hs.at[way, d - 1, p], hr.at[way, d - 1, p], (ring, ring2)[far - 1][way])
        if p == 0:
            send_if(has_prior, copy)
        else:
            send(*copy)

    def hand_over(way, d):
        origin = origin_at(way, d)
        rows = pl.ds(0, 256) if d < half else pl.ds(128 * way, 128)
        send_if(core0, (
            kv.at[origin, 2, rows, :], kv.at[origin, 0, rows, :], ks.at[way, d - 1], hr.at[way, d - 1, 0],
            sibling,
        ))

    def gather_events(d):
        def event(way, p):
            piece = view(origin_at(way, d), p, d, way)
            if p == 0:
                @pl.when(jnp.logical_not(first))
                def _():
                    wait_recv(piece, hr.at[way, d - 1, p])
            else:
                wait_recv(piece, hr.at[way, d - 1, p])
            if p and d < half:
                gather_send(way, d + 1, p)
            if p == 0 and d % 2 == 0:
                for far in (1, 2):
                    if d + far <= half:
                        gather_send(way, d + far, 0, far)
            if p == 2:
                hand_over(way, d)

        return [functools.partial(event, way, p) for p in (2, 1, 0) for way in range(2)]

    for p in (2, 1):
        for hd2 in range(4):
            wait_recv(kv.at[y, p, pl.ds(hd2 * 64, 64), :], fr.at[0, (p - 1) * 4 + hd2])
        wait_recv(kv.at[y, p, pl.ds(256, 16), :], fr.at[3, p - 1])
        for way in range(2):
            gather_send(way, 1, p)
        if p == 2:
            block, prior = (kv.at[y, i, pl.ds(0, 256), :] for i in (2, 0))
            send_if(gives_prior, (block, prior, os, orr, heir))
            send_if(core0, (block, prior, os, orr, sibling))
    token_rows = pl.ds(pl.multiple_of(hd * 32, 32), 32)
    for n, (device, kvh2, x2, me) in enumerate(forward):
        q_cols = pl.ds(pl.multiple_of(kvh2 * width, D), width)
        send(q_ref.at[:, q_cols], qbuf.at[s, token_rows, :], fs.at[1, n], fr.at[1, s * 4 + hd], device, me)
        send(go_ref.at[:, q_cols], gbuf.at[s, token_rows, :], fs.at[2, n], fr.at[2, s * 4 + hd], device, me)


    for device, kvh2, x2, me in forward:
        if me is None:
            pl.semaphore_signal(ready, inc=1, device_id=device, device_id_type=MESH)
        else:
            @pl.when(jnp.logical_not(me))
            def _(device=device):
                pl.semaphore_signal(ready, inc=1, device_id=device, device_id_type=MESH)

    @pl.when(jnp.logical_not(first))
    def _():
        wait_recv(kv.at[y, 0, pl.ds(0, 256), :], orr)

    for far in (1, 2):
        for way in range(2):
            gather_send(way, far, 0, far)
    for d in range(1, half - 1):
        for event in gather_events(d):
            event()

    for s2 in range(2):
        for hd2 in range(4):
            wait_recv(qbuf.at[s2, pl.ds(hd2 * 32, 32), :], fr.at[1, s2 * 4 + hd2])
            wait_recv(gbuf.at[s2, pl.ds(hd2 * 32, 32), :], fr.at[2, s2 * 4 + hd2])
        for g in range(group):
            cols = slice(g * D, (g + 1) * D)
            for src, rows_ref, t_ref in ((qbuf, qrow, q_t), (gbuf, grow, g_t)):
                piece = src[s2, :, cols]
                rows_ref[s2, cols, :] = piece
                t_ref[s2, :, cols] = piece.T

    key_off = lax.rem(lax.broadcasted_iota(jnp.int32, (128, 128), 0), RUN).astype(F32)
    row_off = lax.rem(lax.broadcasted_iota(jnp.int32, (8, 128), 1), RUN).astype(F32)

    penalty = jnp.where(first, -NEG, 0.0)

    def rows_of(origin, qb, which):
        at = [pl.ds(hd2 * 64 + which * 32, 32) for hd2 in range(4)]
        return jnp.concatenate([kv[origin, qb + p, rows, :] for p in range(2) for rows in at], axis=0)

    def forward_chunk(origin):
        for qb in range(2):
            keys, vals = rows_of(origin, qb, 0), rows_of(origin, qb, 1)
            runs = kv[origin, qb + 1, pl.ds(256, 16), :].astype(F32)[:1, :]
            key_pos = jnp.broadcast_to(runs, (128, 128)).T * RUN + key_off
            row_runs = kv[y, qb + 1, pl.ds(256, 16), :].astype(F32)[:1, :]
            allowed = key_pos <= row_runs * RUN + row_off[:1, :]
            for tile in range(0, width, TILE):
                cols = slice(tile, tile + TILE)
                scores = dot(keys, q_t[qb, :, cols])
                prior = scores[:128]
                near = jnp.concatenate(
                    [jnp.where(allowed, scores[128:, g:g + D], NEG) for g in range(0, TILE, D)], axis=1
                )
                prior_top = jnp.max(prior, axis=0, keepdims=True)
                if qb == 0:
                    prior_top = prior_top - penalty
                old = mrun[qb, :, cols]
                top = jnp.maximum(old, jnp.maximum(prior_top, jnp.max(near, axis=0, keepdims=True)))
                mrun[qb, :, cols] = top
                mst[origin, qb, :, cols] = top
                shift = top * EXP_SCALE
                prior_shift = shift + penalty if qb == 0 else shift
                probs = jnp.concatenate(
                    [jnp.exp2(prior * EXP_SCALE - prior_shift), jnp.exp2(near * EXP_SCALE - shift)], axis=0
                )
                faded = jnp.exp2((old - top) * EXP_SCALE)
                lrun[qb, :, cols] = lrun[qb, :, cols] * faded + sum8(probs)
                pst[origin, qb, :, cols] = probs.astype(BF16)
                dprobs = dot(vals, g_t[qb, :, cols])
                drun[qb, :, cols] = drun[qb, :, cols] * faded + sum8(probs * dprobs)

    def chunk_at(d, j):
        return lax.rem(y + ny + (1 - 2 * j) * d, ny)

    def between(events, work, jobs):
        for i, event in enumerate(events):
            event()
            for job in jobs[i * len(jobs) // len(events):(i + 1) * len(jobs) // len(events)]:
                work(*job)

    def forward_at(d, j):
        forward_chunk(chunk_at(d, j))

    between(gather_events(half - 1), forward_at, [(0, 0)] + [(d, j) for d in range(1, half - 1) for j in range(2)])
    forward_at(half - 1, 0)
    last = gather_events(half)
    for event in last[:2]:
        event()
    forward_at(half - 1, 1)
    for event in last[2:]:
        event()
    forward_at(half, 0)

    for qb in range(2):
        inverse = 1.0 / jnp.sum(lrun[qb], axis=0, keepdims=True)
        delta = jnp.sum(drun[qb], axis=0, keepdims=True) * inverse
        lrun[qb] = jnp.broadcast_to(inverse, lrun.shape[1:])
        drun[qb] = jnp.broadcast_to(delta, drun.shape[1:])

    def backward_chunk(d, j):
        origin = chunk_at(d, j)

        for qb in range(2):
            keys, vals = rows_of(origin, qb, 0), rows_of(origin, qb, 1)
            probs16, dscores16 = [], []
            for tile in range(0, width, TILE):
                cols = slice(tile, tile + TILE)
                weight = jnp.exp2((mst[origin, qb, :, cols] - mrun[qb, :, cols]) * EXP_SCALE) * lrun[qb, :1, cols]
                probs = pst[origin, qb, :, cols].astype(F32) * weight
                dprobs = dot(vals, g_t[qb, :, cols])
                probs16.append(probs.astype(BF16))
                dscores16.append((probs * (dprobs - drun[qb, :1, cols])).astype(BF16))
            dscores = jnp.concatenate(dscores16, axis=1)
            acc[origin, qb, 1] = dot(jnp.concatenate(probs16, axis=1), grow[qb])
            acc[origin, qb, 0] = dot(dscores, qrow[qb])
            dq_t[qb] += dot(keys.T, dscores)

        @pl.when(core1)
        def _():
            sib_out[origin] = acc[origin, 0, :, :128, :].astype(BF16)

        send_if(core1, (sib_out.at[origin], sib_in.at[origin], ss.at[d, j], sr.at[d, j], sibling))

    def term(d, j, p, which):
        origin = chunk_at(d, j)
        if p == 0:
            return acc[origin, 0, which, :128, :]
        if p == 1:
            return acc[origin, 0, which, 128:, :] + acc[origin, 1, which, :128, :]
        mine = acc[origin, 1, which, 128:, :]
        return mine + jnp.where(core0, sib_in[origin, which].astype(F32), 0.0)

    def from_sibling(d, j):
        @pl.when(core0)
        def _():
            wait_recv(sib_in.at[chunk_at(d, j)], sr.at[d, j])

    def scatter(n, way, p):
        d = half - n
        if n == 1:
            wait_recv(rbuf.at[way, 0, p, way], rr.at[way, 0, p])
        elif n > 1:
            wait_recv(rbuf.at[way, n - 1, p], rr.at[way, n - 1, p])
        for which in range(2):
            if n == 0 and which != way:
                continue
            total = term(d, way if n else 0, p, which)
            if n > 1 or n == 1 and which == way:
                total = total + rbuf[way, n - 1, p, which].astype(F32)
            part[way, n, p, which] = total.astype(BF16)

    def scatter_events(n):
        def event(way, p):
            if p == 2 and (n or not way):
                from_sibling(half - n, way)
            at = (way, n, p) if n else (way, n, p, way)
            copy = (part.at[at], rbuf.at[at], rs.at[way, n, p], rr.at[way, n, p], ring[way])
            if p == 0:
                @pl.when(has_prior)
                def _():
                    scatter(n, way, p)

                send_if(has_prior, copy)
            else:
                scatter(n, way, p)
                send(*copy)

        return [functools.partial(event, way, p) for p in range(3) for way in range(2)]

    backward_chunk(half, 0)
    for event in scatter_events(0):
        event()
    for n in range(1, half):
        for d in (half - 1, half - 2) if n == 1 else (half - n - 1,):
            for j in range(2 if d else 1):
                backward_chunk(d, j)
        if n == half - 1:
            for s2 in range(2):
                for g in range(group):
                    cols = slice(g * D, (g + 1) * D)
                    gq_out[s2, :, cols] = dq_t[s2, :, cols].T.astype(BF16)
            pl.semaphore_wait(ready, 8 - own.astype(jnp.int32))
            q_cols = pl.ds(pl.multiple_of(kvh * width, D), width)
            for m, (device, hd2, s2, me) in enumerate(back):
                rows = pl.ds(pl.multiple_of(hd2 * 32, 32), 32)
                send(gq_out.at[s2, rows, :], gq_ref.at[:, q_cols], bs.at[1, m], br.at[1, kvh], device, me)
        for event in scatter_events(n):
            event()

    def finish(p):
        for way in range(2):
            wait_recv(rbuf.at[way, half - 1, p], rr.at[way, half - 1, p])
        for which in range(2):
            total = term(0, 0, p, which)
            total = total + rbuf[0, half - 1, p, which].astype(F32) + rbuf[1, half - 1, p, which].astype(F32)
            for hd2 in range(4):
                kv_out[p, hd2, pl.ds(which * 32, 32), :] = total[hd2 * 32:(hd2 + 1) * 32].astype(BF16)

    @pl.when(has_prior)
    def _():
        finish(0)

    send_if(has_prior, *(
        (kv_out.at[0, hd2], prior_in.at[kvh], ps.at[hd2], pr.at[kvh], device) for device, hd2 in owners
    ))
    for p in (1, 2):
        if p == 2:
            from_sibling(0, 0)
        finish(p)
        for m, (device, hd2, s2, me) in enumerate(back):
            if s2 == p - 1:
                send(kv_out.at[p, hd2], kv_in.at[kvh], bs.at[0, m], br.at[0, kvh], device, me)

    def results(with_prior):
        for h in range(KVH):
            both = kv_in[h]
            if with_prior:
                both = (both.astype(F32) + prior_in[h].astype(F32)).astype(BF16)
            cols = slice(h * D, (h + 1) * D)
            gk_ref[:, cols] = both[:32]
            gv_ref[:, cols] = both[32:]

    for h in range(KVH):
        wait_recv(gq_ref.at[:, pl.ds(h * width, width)], br.at[1, h])
        wait_recv(kv_in.at[h], br.at[0, h])

    @pl.when(owns_prior)
    def _():
        for h in range(KVH):
            wait_recv(prior_in.at[h], pr.at[h])
        results(True)

    @pl.when(jnp.logical_not(owns_prior))
    def _():
        results(False)

    for copy, condition in sent:
        if condition is None:
            copy.wait_send()
        else:
            @pl.when(condition)
            def _(copy=copy):
                copy.wait_send()


def on_device(queries, keys, values, grad_out, positions):
    ny, nzh = lax.axis_size("inner"), lax.axis_size("outer") // NX
    rows, width = queries.shape
    group = width // (KVH * D)
    half = ny // 2
    lanes = group * D
    anywhere = pl.BlockSpec(memory_space=pl.ANY)
    vmem = pl.BlockSpec(memory_space=pltpu.VMEM)
    dma = pltpu.SemaphoreType.DMA
    grad_query, grad_key, grad_value = pl.pallas_call(
        functools.partial(kernel, ny, nzh, group),
        out_shape=tuple(jax.ShapeDtypeStruct(a.shape, BF16) for a in (queries, keys, values)),
        in_specs=[anywhere] * 4 + [vmem],
        out_specs=(anywhere, vmem, vmem),
        scratch_shapes=[
            pltpu.VMEM((32, KVH * D), BF16),
            pltpu.VMEM((32, KVH * D), BF16),
            pltpu.VMEM((KVH, 64, D), BF16),
            pltpu.VMEM((16, 128), BF16),
            pltpu.VMEM((ny, 3, 272, D), BF16),
            pltpu.VMEM((2, 128, lanes), BF16),
            pltpu.VMEM((2, 128, lanes), BF16),
            pltpu.VMEM((2, lanes, D), BF16),
            pltpu.VMEM((2, lanes, D), BF16),
            pltpu.VMEM((2, D, lanes), BF16),
            pltpu.VMEM((2, D, lanes), BF16),
            pltpu.VMEM((ny, 2, 256, lanes), BF16),
            pltpu.VMEM((ny, 2, 1, lanes), F32),
            pltpu.VMEM((2, 1, lanes), F32),
            pltpu.VMEM((2, 8, lanes), F32),
            pltpu.VMEM((2, 8, lanes), F32),
            pltpu.VMEM((2, D, lanes), F32),
            pltpu.VMEM((ny, 2, 2, 256, D), F32),
            pltpu.VMEM((2, half, 3, 2, 128, D), BF16),
            pltpu.VMEM((2, half, 3, 2, 128, D), BF16),
            pltpu.VMEM((ny, 2, 128, D), BF16),
            pltpu.VMEM((ny, 2, 128, D), BF16),
            pltpu.VMEM((3, 4, 64, D), BF16),
            pltpu.VMEM((KVH, 64, D), BF16),
            pltpu.VMEM((KVH, 64, D), BF16),
            pltpu.VMEM((2, 128, lanes), BF16),
            dma((2,)),
            dma((4, 8)), dma((4, 8)),
            dma, dma,
            dma((2, half)),
            dma((2, half, 3)), dma((2, half, 3)),
            dma((2, half, 3)), dma((2, half, 3)),
            dma((half + 1, 2)), dma((half + 1, 2)),
            dma((2, 8)), dma((2, 8)),
            dma((4,)), dma((8,)),
            pltpu.SemaphoreType.REGULAR,
        ],
        compiler_params=pltpu.CompilerParams(
            collective_id=0, has_side_effects=True, vmem_limit_bytes=56 * 1024 * 1024
        ),
        name="banded_backward",
    )(queries, keys, values, grad_out, positions.reshape(1, -1))
    scaled = [(a.astype(F32) * SCALE).astype(BF16) for a in (grad_query, grad_key)]
    return (*scaled, grad_value)


def solution(mesh):
    tokens = P(("outer", "inner", "head"), None)
    return jax.shard_map(
        on_device,
        mesh=mesh,
        in_specs=(tokens, tokens, tokens, tokens, P(("outer", "inner"))),
        out_specs=(tokens, tokens, tokens),
        check_vma=False,
    )
```
